256 devices in a mesh: dp: 4 (over x_lo, core), cp: 64 (over z, y, x_hi).
Axes of the slice: x: 4 (x_hi: 2, x_lo: 2; x = x_hi * 2 + x_lo), y: 4, z: 8, core: 2. Of those that a mesh axis runs over, the one named last changes fastest.
Arguments:
- q_raw: bfloat16 [32768, 4096], P(('dp', 'cp')), may hold values from -60 to 60
- k_raw: bfloat16 [32768, 512], P(('dp', 'cp')), may hold values from -60 to 60
- values: bfloat16 [32768, 512], P(('dp', 'cp')), may hold values from -6 to 6
- loss_grad: bfloat16 [32768, 4096], P(('dp', 'cp')), may hold values from -6 to 6
- send_order: int32 [256, 128], P(('dp', 'cp')), may hold values from 0 to 127, each once within a row
- doc_blocks: int32 [4, 64], P('dp', 'cp'), may hold values from 0 to 13, never falling along the last dimension, each value on 1 to 5 neighbouring positions
- gain_q: float32 [128], replicated, may hold values from 0.6 to 4.6
- gain_k: float32 [128], replicated, may hold values from 0.6 to 4.6
Outputs:
- attn_out: bfloat16 [32768, 4096], P(('dp', 'cp'))
- dq_raw: bfloat16 [32768, 4096], P(('dp', 'cp'))
- dk_raw: bfloat16 [32768, 512], P(('dp', 'cp'))
- dv_out: bfloat16 [32768, 512], P(('dp', 'cp'))
- dgain_q: float32 [128], replicated
- dgain_k: float32 [128], replicated
The draws below stay inside these ranges and needn't reach their ends.
Inputs may be any that keep to these rules, and one draw needn't show every extreme that they name: `send_order`: each row is a permutation of 0 to 127. `doc_blocks`: within each row ids never fall, every id 0 to 13 occurs, each document covers 1 to 5 consecutive blocks, and some document covers exactly 5.
All inputs are finite; a program needn't handle non-finite values.
Results may differ from the reference program's by a relative error of at most 0.033.
The reference program's roundings to bfloat16 on the way count: a program that leaves them out, or rounds other values in their place, can miss the bound.
Values may be sent and summed in bfloat16 or wider, within the bound.
No kernel may reach another device: no remote copies, remote signals or barrier semaphores. Data moves between devices by JAX's collectives and lax.ppermute only.
A program may use at most 128 MiB of HBM per device.

```python
import math
import jax
import jax.numpy as jnp
import numpy as np
from jax import lax

HEADS = 32
KV_HEADS = 4
D_HEAD = 128
BLOCK = 128
MOST_BLK = 5
TOK_DEV = 128
ROWS_PEER = 32
GROUP_BLK = 64
DOCS = 14
TOKENS = 32768
N_DP = 4
N_CP = 64


def shared_keys(key):
    return jnp.clip(jax.random.normal(key, (TOKENS, KV_HEADS, D_HEAD), jnp.float32), -6.0, 6.0)


def draw_k_raw(key, part):
    base = shared_keys(key)
    return base.reshape(TOKENS, KV_HEADS * D_HEAD).astype(jnp.bfloat16)


def draw_q_raw(key, part):
    key = jax.random.fold_in(key, 3)
    fresh = jnp.clip(jax.random.normal(key, (TOKENS, HEADS, D_HEAD), jnp.float32), -6.0, 6.0)
    return fresh.reshape(TOKENS, HEADS * D_HEAD).astype(jnp.bfloat16)


def draw_gain_q(key, part):
    key = jax.random.fold_in(key, 11)
    return jax.random.uniform(key, (D_HEAD,), jnp.float32, 0.6, 1.6)


def draw_gain_k(key, part):
    key = jax.random.fold_in(key, 13)
    return jax.random.uniform(key, (D_HEAD,), jnp.float32, 0.6, 1.6)


def levels(key, shape, split, least, top_value):
    loudness, own = 1.0, jax.random.fold_in(key, 6)
    for dim, shards_of in split:
        steps = jnp.exp(jax.random.uniform(jax.random.fold_in(own, dim), (shards_of,), jnp.float32, least / len(split), top_value / len(split)))
        loudness = loudness * jnp.repeat(steps, shape[dim] // shards_of).reshape([-1 if axis == dim else 1 for axis in range(len(shape))])
    return loudness


def split_up(number_of, total, bound, slope):
    weights = [(1 << 20) // math.isqrt(grade ** slope) + 1 for grade in range(2, number_of + 1)]
    surplus, counts = total - bound - (number_of - 1), [1] * (number_of - 1)
    while surplus > 0:
        movable = [i for i in range(number_of - 1) if counts[i] < bound]
        whole, left = sum([weights[i] for i in movable]), surplus
        for i in movable:
            extra = min(bound - counts[i], max(1, left * weights[i] // whole), surplus)
            counts[i] = counts[i] + extra
            surplus = surplus - extra
    return np.array([bound] + counts)


def ragged(stream_key, number_of, total, limit, lean):
    if number_of == 2:
        one = jax.random.randint(stream_key, (), max(1, total - limit), min(limit, total - 1) + 1)
        return jnp.stack([one, total - one])
    tallies = jnp.asarray(split_up(number_of, total, limit, lean), jnp.int32)
    pairs = (number_of - 1) // 2
    source_of, sink = tallies[1:1 + 2 * pairs:2], tallies[2:2 + 2 * pairs:2]
    margin = jnp.minimum(source_of - 1, limit - sink)
    shifted = jax.random.randint(jax.random.fold_in(stream_key, 1), (pairs,), 0, 1 << 20) % (margin + 1)
    tallies = tallies.at[1:1 + 2 * pairs:2].set(source_of - shifted).at[2:2 + 2 * pairs:2].set(sink + shifted)
    return tallies[jax.random.permutation(jax.random.fold_in(stream_key, 2), number_of)]


def gaussian(stream_key, shape, width, bound, cuts=(), held_as=jnp.bfloat16):
    entries = jax.random.normal(stream_key, shape, jnp.float32) * width
    if len(cuts) > 0:
        entries = levels(stream_key, shape, cuts, -0.22, 0.18) * entries
    return jnp.clip(entries, min=-bound, max=bound).astype(held_as)


def setup_inputs(seed: int = 0) -> dict:
    keys = jax.random.split(jax.random.key(seed), 9)
    return {
        "q_raw": draw_q_raw(jax.random.fold_in(keys[8], 71), 0),
        "k_raw": draw_k_raw(jax.random.fold_in(keys[8], 71), 0),
        "values": gaussian(keys[2], (TOKENS, KV_HEADS * D_HEAD), 1.0, 6.0, ((0, 256),)),
        "loss_grad": gaussian(keys[3], (TOKENS, HEADS * D_HEAD), 1.0, 6.0, ((0, 256),)),
        "send_order": jax.vmap(lambda own: jax.random.permutation(own, TOK_DEV))(jax.random.split(keys[4], (N_DP * N_CP))).reshape((N_DP * N_CP, TOK_DEV)).astype(jnp.int32),
        "doc_blocks": jax.vmap(lambda own: jnp.searchsorted(jnp.cumsum(ragged(own, DOCS, GROUP_BLK, MOST_BLK, 2)), jnp.arange(GROUP_BLK), side="right"))(jax.random.split(keys[5], N_DP)).reshape((N_DP, GROUP_BLK)).astype(jnp.int32),
        "gain_q": draw_gain_q(jax.random.fold_in(keys[8], 71), 0),
        "gain_k": draw_gain_k(jax.random.fold_in(keys[8], 71), 0),
    }


EPSILON = 1e-06
THETA = 1000000.0
NEGATIVE = -1e+30

def normalize(raw_rows, gain_vec, head_count):
    values_f = raw_rows.astype(jnp.float32).reshape(raw_rows.shape[0], head_count, -1)
    inv_norm = lax.rsqrt(lax.optimization_barrier(jnp.mean(values_f * values_f, axis=-1, keepdims=True)) + EPSILON)
    unit_vec = values_f * inv_norm
    return (unit_vec, inv_norm, unit_vec * gain_vec)

def rope_tables(position, head_dim):
    half_dim = head_dim // 2
    frequency = THETA ** (-(jnp.arange(half_dim, dtype=jnp.float32) * 2.0 / head_dim))
    angles = position.astype(jnp.float32)[:, None] * frequency[None, :]
    return (jnp.cos(angles)[:, None, :], jnp.sin(angles)[:, None, :])

def rotate(vectors, cosine, sine_tab):
    half_dim = vectors.shape[-1] // 2
    leading = vectors[..., :half_dim]
    trailing = vectors[..., half_dim:]
    return jnp.concatenate([leading * cosine - trailing * sine_tab, trailing * cosine + leading * sine_tab], axis=-1)

def unrotate(cotangent, cosine, sine_tab):
    half_dim = cotangent.shape[-1] // 2
    leading = cotangent[..., :half_dim]
    trailing = cotangent[..., half_dim:]
    return jnp.concatenate([leading * cosine + trailing * sine_tab, trailing * cosine - leading * sine_tab], axis=-1)

def norm_back(cotangent, unit_vec, inv_norm, gain_vec):
    scaled_grad = cotangent * gain_vec
    inner_sum = lax.optimization_barrier(jnp.mean(scaled_grad * unit_vec, axis=-1, keepdims=True))
    return (inv_norm * (scaled_grad - unit_vec * inner_sum), lax.optimization_barrier(jnp.sum(cotangent * unit_vec, axis=(0, 1))))

def group_pass(group, q_raw, k_raw, values, loss_grad, send_order, doc_blocks, gain_q, gain_k):
    seq_len = N_CP * TOK_DEV
    group_size = HEADS // KV_HEADS
    inv_root = 1.0 / math.sqrt(D_HEAD)
    route = send_order.reshape(N_DP, N_CP, TOK_DEV)
    columns = lax.dynamic_slice_in_dim(route, group * ROWS_PEER, ROWS_PEER, 2)
    source_a = jnp.arange(N_DP, dtype=jnp.int32)[:, None, None]
    source_c = jnp.arange(N_CP, dtype=jnp.int32)[None, :, None]

    def pick(array):
        shaped = array.reshape(N_DP, N_CP, TOK_DEV, array.shape[1])
        taken = shaped[source_a, source_c, columns]
        return jnp.transpose(taken, (1, 0, 2, 3)).reshape(seq_len, array.shape[1])
    q_rows = pick(q_raw)
    k_rows = pick(k_raw)
    v_rows = pick(values)
    g_rows = pick(loss_grad)
    doc_ids = doc_blocks[group]
    first_block = lax.optimization_barrier(jnp.sum((doc_ids[None, :] < doc_ids[:, None]).astype(jnp.int32), axis=1))
    position = jnp.arange(seq_len, dtype=jnp.int32) - jnp.repeat(first_block, BLOCK) * BLOCK
    cosine, sine_tab = rope_tables(position, D_HEAD)
    q_unit, q_norm, q_scaled = normalize(q_rows, gain_q, HEADS)
    k_unit, k_norm, k_scaled = normalize(k_rows, gain_k, KV_HEADS)
    queries = rotate(q_scaled, cosine, sine_tab).astype(jnp.bfloat16).reshape(seq_len, KV_HEADS, group_size, D_HEAD)
    keys_rot = rotate(k_scaled, cosine, sine_tab).astype(jnp.bfloat16)
    values_kv = v_rows.reshape(seq_len, KV_HEADS, D_HEAD)
    g_heads = g_rows.reshape(seq_len, KV_HEADS, group_size, D_HEAD)
    stat_shape = (KV_HEADS, group_size, BLOCK)

    def block_pass(carried, block_idx):
        dk_acc, dv_acc = carried
        q_block = lax.dynamic_slice_in_dim(queries, block_idx * BLOCK, BLOCK, 0).astype(jnp.float32)
        g_block = lax.dynamic_slice_in_dim(g_heads, block_idx * BLOCK, BLOCK, 0).astype(jnp.float32)
        query_index = block_idx * BLOCK + jnp.arange(BLOCK, dtype=jnp.int32)

        def key_side(distance):
            key_block = block_idx - distance.astype(jnp.int32)
            active = (key_block >= 0) & (doc_ids[jnp.maximum(key_block, 0)] == doc_ids[block_idx])
            offset = jnp.maximum(key_block, 0) * BLOCK
            key_index = key_block * BLOCK + jnp.arange(BLOCK, dtype=jnp.int32)
            allowed = key_index[None, :] <= query_index[:, None]
            return (active, offset, allowed)

        def scores_at(offset):
            keys_block = lax.dynamic_slice_in_dim(keys_rot, offset, BLOCK, 0).astype(jnp.float32)
            return jnp.einsum('tkgd,ukd->kgtu', q_block, keys_block) * inv_root

        def max_step(distance, row_max):
            active, offset, allowed = key_side(distance)

            def taken(operands):
                scores = scores_at(operands[0])
                return lax.optimization_barrier(jnp.max(jnp.where(operands[1][None, None], scores, NEGATIVE), axis=-1))

            def skipped(operands):
                return jnp.full(stat_shape, NEGATIVE, jnp.float32)
            return jnp.maximum(row_max, lax.cond(active, taken, skipped, (offset, allowed)))
        row_max = lax.fori_loop(0, MOST_BLK, max_step, jnp.full(stat_shape, NEGATIVE, jnp.float32))

        def sum_step(distance, state):
            row_sum, out_acc = state
            active, offset, allowed = key_side(distance)

            def taken(operands):
                scores = scores_at(operands[0])
                weights = jnp.where(operands[1][None, None], jnp.exp(scores - row_max[..., None]), 0.0)
                values_block = lax.dynamic_slice_in_dim(values_kv, operands[0], BLOCK, 0).astype(jnp.float32)
                rounded = weights.astype(jnp.bfloat16).astype(jnp.float32)
                return (lax.optimization_barrier(jnp.sum(weights, axis=-1)), jnp.einsum('kgtu,ukd->tkgd', rounded, values_block))

            def skipped(operands):
                return (jnp.zeros(stat_shape, jnp.float32), jnp.zeros((BLOCK, KV_HEADS, group_size, D_HEAD), jnp.float32))
            add_sum, add_out = lax.cond(active, taken, skipped, (offset, allowed))
            return (row_sum + add_sum, out_acc + add_out)
        row_sum, out_acc = lax.fori_loop(0, MOST_BLK, sum_step, (jnp.zeros(stat_shape, jnp.float32), jnp.zeros((BLOCK, KV_HEADS, group_size, D_HEAD), jnp.float32)))
        out_block = (out_acc / jnp.transpose(row_sum, (2, 0, 1))[..., None]).astype(jnp.bfloat16)
        lse_row = row_max + jnp.log(row_sum)
        delta_row = jnp.transpose(lax.optimization_barrier(jnp.sum(g_block * out_block.astype(jnp.float32), axis=-1)), (1, 2, 0))

        def back_step(distance, state):
            dq_acc, dk_run, dv_run = state
            active, offset, allowed = key_side(distance)

            def taken(operands):
                scores = scores_at(operands[0])
                keys_block = lax.dynamic_slice_in_dim(keys_rot, operands[0], BLOCK, 0).astype(jnp.float32)
                values_block = lax.dynamic_slice_in_dim(values_kv, operands[0], BLOCK, 0).astype(jnp.float32)
                probs = jnp.where(operands[1][None, None], jnp.exp(scores - lse_row[..., None]), 0.0)
                dprobs = jnp.einsum('tkgd,ukd->kgtu', g_block, values_block)
                dscores = (probs * (dprobs - delta_row[..., None])).astype(jnp.bfloat16).astype(jnp.float32)
                probs_b = probs.astype(jnp.bfloat16).astype(jnp.float32)
                dq_part = jnp.einsum('kgtu,ukd->tkgd', dscores, keys_block) * inv_root
                dk_part = jnp.einsum('kgtu,tkgd->ukd', dscores, q_block) * inv_root
                dv_part = jnp.einsum('kgtu,tkgd->ukd', probs_b, g_block)
                return (dq_part, dk_part, dv_part)

            def skipped(operands):
                return (jnp.zeros((BLOCK, KV_HEADS, group_size, D_HEAD), jnp.float32), jnp.zeros((BLOCK, KV_HEADS, D_HEAD), jnp.float32), jnp.zeros((BLOCK, KV_HEADS, D_HEAD), jnp.float32))
            dq_part, dk_part, dv_part = lax.cond(active, taken, skipped, (offset, allowed))
            dk_run = lax.dynamic_update_slice_in_dim(dk_run, lax.dynamic_slice_in_dim(dk_run, offset, BLOCK, 0) + dk_part, offset, 0)
            dv_run = lax.dynamic_update_slice_in_dim(dv_run, lax.dynamic_slice_in_dim(dv_run, offset, BLOCK, 0) + dv_part, offset, 0)
            return (dq_acc + dq_part, dk_run, dv_run)
        dq_block, dk_acc, dv_acc = lax.fori_loop(0, MOST_BLK, back_step, (jnp.zeros((BLOCK, KV_HEADS, group_size, D_HEAD), jnp.float32), dk_acc, dv_acc))
        return ((dk_acc, dv_acc), (out_block, dq_block))
    zeros_kv = jnp.zeros((seq_len, KV_HEADS, D_HEAD), jnp.float32)
    (dk_total, dv_total), (out_blocks, dq_blocks) = lax.scan(block_pass, (zeros_kv, zeros_kv), jnp.arange(GROUP_BLK, dtype=jnp.int32))
    attn_rows = out_blocks.reshape(seq_len, HEADS * D_HEAD)
    dq_rot = dq_blocks.reshape(seq_len, HEADS, D_HEAD)
    dq_rows, gq_part = norm_back(unrotate(dq_rot, cosine, sine_tab), q_unit, q_norm, gain_q)
    dk_rows, gk_part = norm_back(unrotate(dk_total, cosine, sine_tab), k_unit, k_norm, gain_k)
    return (attn_rows, dq_rows.astype(jnp.bfloat16).reshape(seq_len, HEADS * D_HEAD), dk_rows.astype(jnp.bfloat16).reshape(seq_len, KV_HEADS * D_HEAD), dv_total.astype(jnp.bfloat16).reshape(seq_len, KV_HEADS * D_HEAD), gq_part, gk_part)

def reference(q_raw, k_raw, values, loss_grad, send_order, doc_blocks, gain_q, gain_k):

    def one_group(group):
        return group_pass(group, q_raw, k_raw, values, loss_grad, send_order, doc_blocks, gain_q, gain_k)
    attn_rows, dq_rows, dk_rows, dv_rows, gq_parts, gk_parts = lax.map(one_group, jnp.arange(N_DP, dtype=jnp.int32))
    factor = 1.0 / math.sqrt(TOKENS)
    return (attn_rows.reshape(TOKENS, HEADS * D_HEAD), dq_rows.reshape(TOKENS, HEADS * D_HEAD), dk_rows.reshape(TOKENS, KV_HEADS * D_HEAD), dv_rows.reshape(TOKENS, KV_HEADS * D_HEAD), lax.optimization_barrier(jnp.sum(gq_parts, axis=0)) * factor, lax.optimization_barrier(jnp.sum(gk_parts, axis=0)) * factor)
```

```python
import math

import jax
import jax.numpy as jnp
import numpy as np
from jax import lax
from jax.experimental import pallas as pl
from jax.experimental.pallas import tpu as pltpu
from jax.sharding import PartitionSpec as P

REACH = 4
EPSILON = 1e-06
THETA = 1000000.0
NEGATIVE = -1e30
TOK = 128
DIM = 128
KV = 4
GROUP = 8
N_DP = 4
N_CP = 64
ROWS = TOK // N_DP
KEYS = (REACH + 1) * TOK
ID_ROWS = 8
TILE = 256
PAIR = 2 * DIM
WIDE = 2 * GROUP * DIM
INV_ROOT = 1.0 / math.sqrt(DIM)
LOG2E = 1.4426950408889634
BF = jnp.bfloat16
F32 = jnp.float32
VMEM = pl.BlockSpec(memory_space=pltpu.VMEM)
SMEM = pl.BlockSpec(memory_space=pltpu.SMEM)
PARAMS = pltpu.CompilerParams(vmem_limit_bytes=48 * 1024 * 1024)


def tables():
    half = DIM // 2
    frequency = (THETA ** (-(np.arange(half) * 2.0 / DIM))).astype(np.float32)
    angles = np.arange(KEYS, dtype=np.float32)[:, None] * frequency[None, :]
    cosine = np.cos(angles.astype(np.float64)).astype(np.float32)
    sine = np.sin(angles.astype(np.float64)).astype(np.float32)
    return (
        np.concatenate([cosine, cosine], axis=1),
        np.concatenate([-sine, sine], axis=1),
    )


def dot(left, right, left_dim, right_dim):
    return lax.dot_general(
        left, right, (((left_dim,), (right_dim,)), ((), ())), preferred_element_type=F32
    )


def picker(order_ref):
    rows = lax.broadcasted_iota(jnp.int32, (TOK, TOK), 0)
    return jnp.where(rows == order_ref[...], 1.0, 0.0).astype(BF)


def slot_rows(slot):
    place = lax.axis_index("dp") ^ slot
    return pl.ds(pl.multiple_of(place * ROWS, ROWS), ROWS)


def kv_pick(order_ref, k_ref, v_ref, *rest):
    outs, rows_ref = rest[:N_DP], rest[N_DP]
    chosen = picker(order_ref)
    keys = dot(chosen, k_ref[...], 0, 0).astype(BF)
    vals = dot(chosen, v_ref[...], 0, 0).astype(BF)
    for head in range(KV):
        rows_ref[:, head * PAIR : head * PAIR + DIM] = keys[:, head * DIM : (head + 1) * DIM]
        rows_ref[:, head * PAIR + DIM : (head + 1) * PAIR] = vals[:, head * DIM : (head + 1) * DIM]
    for slot in range(N_DP):
        outs[slot][...] = rows_ref[slot_rows(slot), :]


def qg_pick(order_ref, q_ref, g_ref, *rest):
    outs, rows_ref = rest[:N_DP], rest[N_DP]
    chosen = picker(order_ref)
    half = GROUP * DIM
    rows_ref[:, :half] = dot(chosen, q_ref[...], 0, 0).astype(BF)
    rows_ref[:, half:] = dot(chosen, g_ref[...], 0, 0).astype(BF)
    for slot in range(N_DP):
        outs[slot][...] = rows_ref[slot_rows(slot), :]


def kv_join(doc_ref, *rest):
    slots, out_ref = rest[:N_DP], rest[N_DP]
    for slot in range(N_DP):
        out_ref[slot_rows(slot), :] = slots[slot][...]
    width = out_ref.shape[1]
    out_ref[TOK:, :] = jnp.full((ID_ROWS, width), doc_ref[0, 0], jnp.int32).astype(F32).astype(BF)


def same_docs(doc_ref, shards):
    own = doc_ref[0, 0].astype(F32)
    place = lax.axis_index("cp")
    flags = []
    for back in range(1, REACH + 1):
        near = jnp.max(shards[back][TOK : TOK + ID_ROWS, 0:DIM].astype(F32))
        flags.append(jnp.where((near == own) & (place >= back), 1, 0).astype(jnp.int32))
    return flags


def table_rows(block):
    return pl.ds(pl.multiple_of(block * TOK, TOK), TOK)


def turn(vectors, cosine, sine):
    return vectors * cosine + pltpu.roll(vectors, DIM // 2, 1) * sine


def turn_back(vectors, cosine, sine):
    return vectors * cosine - pltpu.roll(vectors, DIM // 2, 1) * sine


def unit_of(raw):
    inv_norm = lax.rsqrt(jnp.mean(raw * raw, axis=-1, keepdims=True) + EPSILON)
    return raw * inv_norm, inv_norm


def attend(doc_ref, *rest):
    slots = rest[:N_DP]
    shards = rest[N_DP : N_DP + REACH + 1]
    cos_ref, sin_ref, gq_ref, gk_ref = rest[N_DP + REACH + 1 : N_DP + REACH + 5]
    outs = rest[N_DP + REACH + 5 :]
    out_ref, dq_ref = outs[:2]
    own_ref = outs[2]
    part_refs = outs[3 : 3 + REACH]
    gain_ref = outs[3 + REACH]
    place_ref = outs[4 + REACH]
    rows_ref, bias_ref = outs[5 + REACH :]
    step = pl.program_id(0)
    flags = same_docs(doc_ref, shards)
    block = flags[0] + flags[1] + flags[2] + flags[3]
    place_ref[0, 0] = block

    @pl.when(step == 0)
    def start():
        gain_ref[...] = jnp.zeros_like(gain_ref)
        for back in range(REACH, 0, -1):
            first = (REACH - back) * TOK
            level = jnp.where(flags[back - 1] > 0, 0.0, NEGATIVE)
            bias_ref[first : first + TOK, :] = jnp.full((TOK, TILE), level, F32)
        key = lax.broadcasted_iota(jnp.int32, (TOK, TILE), 0)
        query = lax.broadcasted_iota(jnp.int32, (TOK, TILE), 1) & (TOK - 1)
        bias_ref[REACH * TOK :, :] = jnp.where(key <= query, 0.0, NEGATIVE)

    for slot in range(N_DP):
        rows_ref[slot_rows(slot), :] = slots[slot][...]
    gain_q = gq_ref[...]
    gain_k = gk_ref[...]
    key_cos, key_sin, key_unit, key_rot, key_val = [], [], [], [], []
    for back in range(REACH, -1, -1):
        where = table_rows(jnp.maximum(block - back, 0))
        cosine, sine = cos_ref[where, :], sin_ref[where, :]
        unit, _ = unit_of(shards[back][:TOK, :DIM].astype(F32))
        key_cos.append(cosine)
        key_sin.append(sine)
        key_unit.append(unit)
        key_rot.append(turn(unit * gain_k, cosine, sine))
        key_val.append(shards[back][:TOK, DIM:])
    rot_f = jnp.concatenate(key_rot, axis=0).astype(BF)
    val_b = jnp.concatenate(key_val, axis=0)
    rot_t = rot_f.T
    val_t = val_b.T
    bias = bias_ref[...]
    own_rows = table_rows(block)
    cosine = jnp.concatenate([cos_ref[own_rows, :]] * (TILE // TOK), axis=0)
    sine = jnp.concatenate([sin_ref[own_rows, :]] * (TILE // TOK), axis=0)
    dk_total = jnp.zeros((KEYS, DIM), F32)
    dv_total = jnp.zeros((KEYS, DIM), F32)
    gq_total = jnp.zeros((8, DIM), F32)
    heads = TILE // TOK
    for first in range(0, GROUP, heads):
        places = [(first + j) * DIM for j in range(heads)]
        raw = jnp.concatenate([rows_ref[:, at : at + DIM] for at in places], axis=0)
        grad = jnp.concatenate(
            [rows_ref[:, GROUP * DIM + at : GROUP * DIM + at + DIM] for at in places], axis=0
        )
        unit, inv_norm = unit_of(raw.astype(F32))
        query = turn(unit * gain_q, cosine, sine).astype(BF)
        scores = dot(rot_f, query, 1, 1) * (INV_ROOT * LOG2E) + bias
        top = jnp.max(scores, axis=0, keepdims=True)
        weights = jnp.exp2(scores - top)
        total = jnp.sum(weights, axis=0, keepdims=True)
        inverse = 1.0 / total
        out_t = (dot(val_t, weights.astype(BF), 1, 0) / total).astype(BF).astype(F32)
        out = out_t.T.astype(BF)
        grad_t = grad.astype(F32).T
        delta = jnp.sum(grad_t * out_t, axis=0, keepdims=True)
        probs = weights * inverse
        dscore = (probs * (dot(val_b, grad, 1, 1) - delta)).astype(BF)
        dq_rot = dot(rot_t, dscore, 1, 0).T * INV_ROOT
        dk_total = dk_total + dot(dscore, query, 1, 0)
        dv_total = dv_total + dot(probs.astype(BF), grad, 1, 0)
        dqn = turn_back(dq_rot, cosine, sine)
        scaled = dqn * gain_q
        inner = jnp.mean(scaled * unit, axis=-1, keepdims=True)
        dq = (inv_norm * (scaled - unit * inner)).astype(BF)
        gq_total = gq_total + jnp.sum((dqn * unit).reshape(TILE // 8, 8, DIM), axis=0)
        for j, at in enumerate(places):
            out_ref[:, at : at + DIM] = out[j * TOK : (j + 1) * TOK]
            dq_ref[:, at : at + DIM] = dq[j * TOK : (j + 1) * TOK]
    dk_total = dk_total * INV_ROOT
    gk_total = jnp.zeros((8, DIM), F32)
    for at, back in enumerate(range(REACH, -1, -1)):
        dk_part = dk_total[at * TOK : (at + 1) * TOK]
        dv_part = dv_total[at * TOK : (at + 1) * TOK]
        dkn = turn_back(dk_part, key_cos[at], key_sin[at])
        gk_total = gk_total + jnp.sum((dkn * key_unit[at]).reshape(TOK // 8, 8, DIM), axis=0)
        target = own_ref if back == 0 else part_refs[back - 1]
        target[:, :DIM] = dk_part.astype(target.dtype)
        target[:, DIM:] = dv_part.astype(target.dtype)
    gain_ref[:, :DIM] += gq_total
    gain_ref[:, DIM:] += gk_total


def finish(place_ref, own_ref, *rest):
    parts = rest[:REACH]
    kv_ref, cos_ref, sin_ref, gk_ref, dk_ref, dv_ref = rest[REACH:]
    where = table_rows(place_ref[0, 0])
    cosine, sine = cos_ref[where, :], sin_ref[where, :]
    gain_k = gk_ref[...]
    for head in range(KV):
        left = head * PAIR
        both = own_ref[:, left : left + PAIR]
        for part in parts:
            both = both + part[:, left : left + PAIR].astype(F32)
        unit, inv_norm = unit_of(kv_ref[:TOK, left : left + DIM].astype(F32))
        scaled = turn_back(both[:, :DIM], cosine, sine) * gain_k
        inner = jnp.mean(scaled * unit, axis=-1, keepdims=True)
        dk_ref[:, head * DIM : (head + 1) * DIM] = (inv_norm * (scaled - unit * inner)).astype(BF)
        dv_ref[:, head * DIM : (head + 1) * DIM] = both[:, DIM:].astype(BF)


def swap(array, slot):
    return lax.ppermute(array, "dp", [(j, j ^ slot) for j in range(N_DP)])


def shifted(array, by):
    return lax.ppermute(array, "cp", [(j, (j + by) % N_CP) for j in range(N_CP)])


def shape(*dims, dtype=BF):
    return jax.ShapeDtypeStruct(dims, dtype)


def body(q_raw, k_raw, values, loss_grad, send_order, doc_blocks, gain_q, gain_k):
    cos_np, sin_np = tables()
    cos_tab, sin_tab = jnp.asarray(cos_np), jnp.asarray(sin_np)
    gain_q = gain_q.reshape(1, DIM)
    gain_k = gain_k.reshape(1, DIM)
    kv_slots = pl.pallas_call(
        kv_pick,
        out_shape=[shape(ROWS, KV * PAIR)] * N_DP,
        in_specs=[VMEM] * 3,
        out_specs=[VMEM] * N_DP,
        scratch_shapes=[pltpu.VMEM((TOK, KV * PAIR), BF)],
        compiler_params=PARAMS,
        name="kv_pick",
    )(send_order, k_raw, values)
    kv_slots = [kv_slots[0]] + [swap(kv_slots[slot], slot) for slot in range(1, N_DP)]
    half = GROUP * DIM
    qg_slots = pl.pallas_call(
        qg_pick,
        grid=(KV,),
        out_shape=[shape(ROWS, KV * WIDE)] * N_DP,
        in_specs=[
            pl.BlockSpec((1, TOK), lambda h: (0, 0)),
            pl.BlockSpec((TOK, half), lambda h: (0, h)),
            pl.BlockSpec((TOK, half), lambda h: (0, h)),
        ],
        out_specs=[pl.BlockSpec((ROWS, WIDE), lambda h: (0, h))] * N_DP,
        scratch_shapes=[pltpu.VMEM((TOK, WIDE), BF)],
        compiler_params=PARAMS,
        name="qg_pick",
    )(send_order, q_raw, loss_grad)
    kv_own = pl.pallas_call(
        kv_join,
        out_shape=shape(TOK + ID_ROWS, KV * PAIR),
        in_specs=[SMEM] + [VMEM] * N_DP,
        out_specs=VMEM,
        compiler_params=PARAMS,
        name="kv_join",
    )(doc_blocks, *kv_slots)
    shards = [kv_own] + [shifted(kv_own, back) for back in range(1, REACH + 1)]
    qg_slots = [qg_slots[0]] + [swap(qg_slots[slot], slot) for slot in range(1, N_DP)]
    whole = lambda h: (0, 0)
    by_head = lambda h: (0, h)
    results = pl.pallas_call(
        attend,
        grid=(KV,),
        out_shape=[
            shape(TOK, KV * half),
            shape(TOK, KV * half),
            shape(TOK, KV * PAIR, dtype=F32),
        ]
        + [shape(TOK, KV * PAIR)] * REACH
        + [shape(8, 2 * DIM, dtype=F32), shape(1, 1, dtype=jnp.int32)],
        in_specs=[SMEM]
        + [pl.BlockSpec((ROWS, WIDE), by_head)] * N_DP
        + [pl.BlockSpec((TOK + ID_ROWS, PAIR), by_head)] * (REACH + 1)
        + [pl.BlockSpec((KEYS, DIM), whole)] * 2
        + [pl.BlockSpec((1, DIM), whole)] * 2,
        out_specs=[
            pl.BlockSpec((TOK, half), by_head),
            pl.BlockSpec((TOK, half), by_head),
            pl.BlockSpec((TOK, PAIR), by_head),
        ]
        + [pl.BlockSpec((TOK, PAIR), by_head)] * REACH
        + [pl.BlockSpec((8, 2 * DIM), whole), SMEM],
        scratch_shapes=[pltpu.VMEM((TOK, WIDE), BF), pltpu.VMEM((KEYS, TILE), F32)],
        compiler_params=PARAMS,
        name="attend",
    )(doc_blocks, *qg_slots, *shards, cos_tab, sin_tab, gain_q, gain_k)
    attn_out, dq_raw, dkv_own = results[:3]
    parts = [shifted(results[2 + back], -back) for back in range(1, REACH + 1)]
    gains, place = results[3 + REACH :]
    gain_row = jnp.sum(gains, axis=0, keepdims=True)
    everyone = lax.all_to_all(
        jnp.broadcast_to(gain_row, (N_DP * N_CP, 2 * DIM)), ("dp", "cp"), 0, 0, tiled=True
    )
    gain_sum = jnp.sum(everyone, axis=0) * (1.0 / math.sqrt(TOK * N_DP * N_CP))
    dk_raw, dv_out = pl.pallas_call(
        finish,
        out_shape=[shape(TOK, KV * DIM)] * 2,
        in_specs=[SMEM] + [VMEM] * (REACH + 5),
        out_specs=[VMEM] * 2,
        compiler_params=PARAMS,
        name="finish",
    )(place, dkv_own, *parts, kv_own, cos_tab, sin_tab, gain_k)
    return attn_out, dq_raw, dk_raw, dv_out, gain_sum[:DIM], gain_sum[DIM:]


def solution(mesh):
    rows = P(("dp", "cp"), None)
    return jax.shard_map(
        body,
        mesh=mesh,
        in_specs=(rows, rows, rows, rows, rows, P("dp", "cp"), P(), P()),
        out_specs=(rows, rows, rows, rows, P(), P()),
        check_vma=False,
    )
```

```python
import math

import jax
import jax.numpy as jnp
import numpy as np
from jax import lax
from jax.experimental import pallas as pl
from jax.experimental.pallas import tpu as pltpu
from jax.sharding import PartitionSpec as P

REACH = 4
EPSILON = 1e-06
THETA = 1000000.0
NEGATIVE = -1e30
TOK = 128
DIM = 128
KV = 4
GROUP = 8
N_DP = 4
N_CP = 64
ROWS = TOK // N_DP
KEYS = (REACH + 1) * TOK
ID_ROWS = 8
TILE = 256
LAG = 1
PAIR = 2 * DIM
WIDE = 2 * GROUP * DIM
INV_ROOT = 1.0 / math.sqrt(DIM)
LOG2E = 1.4426950408889634
BF = jnp.bfloat16
F32 = jnp.float32
blocks = [slice(at * TOK, (at + 1) * TOK) for at in range(REACH + 1)]
VMEM = pl.BlockSpec(memory_space=pltpu.VMEM)
SMEM = pl.BlockSpec(memory_space=pltpu.SMEM)
VLIM = 24
PARAMS = pltpu.CompilerParams(vmem_limit_bytes=VLIM * 1024 * 1024)


def tables():
    half = DIM // 2
    frequency = (THETA ** (-(np.arange(half) * 2.0 / DIM))).astype(np.float32)
    angles = np.arange(KEYS, dtype=np.float32)[:, None] * frequency[None, :]
    cosine = np.cos(angles.astype(np.float64)).astype(np.float32)
    sine = np.sin(angles.astype(np.float64)).astype(np.float32)
    return np.concatenate([cosine, cosine, -sine, sine], axis=1)


def dot(left, right, left_dim, right_dim):
    return lax.dot_general(
        left, right, (((left_dim,), (right_dim,)), ((), ())), preferred_element_type=F32
    )


def picker(order_ref):
    rows = lax.broadcasted_iota(jnp.int32, (TOK, TOK), 0)
    return jnp.where(rows == order_ref[...], 1.0, 0.0).astype(BF)


def slot_rows(slot):
    place = lax.axis_index("dp") ^ slot
    return pl.ds(pl.multiple_of(place * ROWS, ROWS), ROWS)


def kv_pick(order_ref, k_ref, v_ref, *rest):
    outs, rows_ref = rest[:N_DP], rest[N_DP]
    chosen = picker(order_ref)
    keys = dot(chosen, k_ref[...], 0, 0).astype(BF)
    vals = dot(chosen, v_ref[...], 0, 0).astype(BF)
    for head in range(KV):
        rows_ref[:, head * PAIR : head * PAIR + DIM] = keys[:, head * DIM : (head + 1) * DIM]
        rows_ref[:, head * PAIR + DIM : (head + 1) * PAIR] = vals[:, head * DIM : (head + 1) * DIM]
    for slot in range(N_DP):
        outs[slot][...] = rows_ref[slot_rows(slot), :]


def qg_pick(order_ref, q_ref, g_ref, *rest):
    q_outs, g_outs, rows_ref = rest[:N_DP], rest[N_DP : 2 * N_DP], rest[2 * N_DP]
    chosen = picker(order_ref)
    half = GROUP * DIM
    rows_ref[:, :half] = dot(chosen, q_ref[...], 0, 0).astype(BF)
    rows_ref[:, half:] = dot(chosen, g_ref[...], 0, 0).astype(BF)
    for slot in range(N_DP):
        q_outs[slot][...] = rows_ref[slot_rows(slot), :half]
        g_outs[slot][...] = rows_ref[slot_rows(slot), half:]


def kv_join(doc_ref, *rest):
    slots, out_ref = rest[:N_DP], rest[N_DP]
    for slot in range(N_DP):
        out_ref[slot_rows(slot), :] = slots[slot][...]
    width = out_ref.shape[1]
    out_ref[TOK:, :] = jnp.full((ID_ROWS, width), doc_ref[0, 0], jnp.int32).astype(F32).astype(BF)


def same_docs(doc_ref, shards):
    own = doc_ref[0, 0].astype(F32)
    place = lax.axis_index("cp")
    flags = []
    for back in range(1, REACH + 1):
        near = jnp.max(shards[back][TOK : TOK + ID_ROWS, 0:DIM].astype(F32))
        flags.append(jnp.where((near == own) & (place >= back), 1, 0).astype(jnp.int32))
    return flags


def flip_angles(table_ref, block):
    first = pl.multiple_of(block * TOK, TOK)
    second = pl.multiple_of(block * TOK + KEYS, TOK)
    return table_ref[:, pl.ds(first, TOK)], table_ref[:, pl.ds(second, TOK)]


def half_swap(array):
    return jnp.concatenate([array[DIM // 2 :], array[: DIM // 2]], axis=0)


def angles_of(table_ref, block):
    rows = table_ref[pl.ds(pl.multiple_of(block * TOK, TOK), TOK), :]
    return rows[:, :DIM], rows[:, DIM:]


def turn(vectors, cosine, sine):
    return vectors * cosine + pltpu.roll(vectors, DIM // 2, 1) * sine


def turn_back(vectors, cosine, sine):
    return vectors * cosine - pltpu.roll(vectors, DIM // 2, 1) * sine


def unit_of(raw):
    inv_norm = lax.rsqrt(jnp.mean(raw * raw, axis=-1, keepdims=True) + EPSILON)
    return raw * inv_norm, inv_norm


def query_unit(*refs):
    slots = refs[:N_DP]
    table_ref, flip_ref, unit_ref, norm_ref, table_out, flip_out, rows_ref = refs[N_DP:]
    table_out[...] = table_ref[...]
    flip_out[...] = flip_ref[...]
    for slot in range(N_DP):
        rows_ref[slot_rows(slot), :] = slots[slot][...]
    for at in range(0, GROUP * DIM, DIM):
        raw = rows_ref[:, at : at + DIM].astype(F32).T
        inv_norm = lax.rsqrt(jnp.mean(raw * raw, axis=0, keepdims=True) + EPSILON)
        unit_ref[:, at : at + DIM] = raw * inv_norm
        norm_ref[:, at : at + DIM] = jnp.broadcast_to(inv_norm, (8, DIM))


def forward(doc_ref, *rest):
    unitq_ref = rest[0]
    shards = rest[1 : REACH + 2]
    table_ref, flip_ref, gq_ref, gk_ref = rest[REACH + 2 : REACH + 6]
    out_ref, again_ref, prob_ref, query_ref, rot_ref, unit_ref, place_ref = rest[REACH + 6 :]
    flags = same_docs(doc_ref, shards)
    block = flags[0] + flags[1] + flags[2] + flags[3]
    place_ref[0, 0] = block
    gain_q = jnp.broadcast_to(gq_ref[...], (TOK, DIM)).T
    gain_k = gk_ref[...]
    own_cos, own_sin = flip_angles(flip_ref, block)
    key_rot, key_val = [], []
    for at, back in enumerate(range(REACH, -1, -1)):
        cosine, sine = angles_of(table_ref, jnp.maximum(block - back, 0))
        unit, _ = unit_of(shards[back][:TOK, :DIM].astype(F32))
        turned = turn(unit * gain_k, cosine, sine).astype(BF)
        unit_ref[blocks[at], :] = unit
        rot_ref[blocks[at], :] = turned
        key_rot.append(turned)
        key_val.append(shards[back][:TOK, DIM:])
    rot_f = jnp.concatenate(key_rot, axis=0)
    val_t = jnp.concatenate(key_val, axis=0).T
    levels = [jnp.where(flags[back - 1] > 0, 0.0, NEGATIVE) for back in range(REACH, 0, -1)]
    key = lax.broadcasted_iota(jnp.int32, (TOK, TILE), 0)
    query = lax.broadcasted_iota(jnp.int32, (TOK, TILE), 1) & (TOK - 1)
    causal = key <= query
    heads = TILE // TOK

    def ready(first):
        places = [(first + j) * DIM for j in range(heads)]
        turned = []
        for at in places:
            scaled = unitq_ref[:, at : at + DIM] * gain_q
            query_t = scaled * own_cos + half_swap(scaled) * own_sin
            turned.append(query_t.astype(BF))
            query_ref[:, at : at + DIM] = query_t.T.astype(BF)
        return places, dot(rot_f, jnp.concatenate(turned, axis=1), 1, 0)

    def soft(state):
        places, scores = state
        last = jnp.where(causal, scores[blocks[REACH]], NEGATIVE)
        parts = [scores[blocks[at]] for at in range(REACH)] + [last]
        tops = [jnp.max(part, axis=0, keepdims=True) for part in parts]
        top = tops[REACH]
        for at in range(REACH):
            top = jnp.maximum(top, tops[at] + levels[at])
        top = top * (INV_ROOT * LOG2E)
        weights, total = [], 0.0
        for at in range(REACH + 1):
            shift = top if at == REACH else top - levels[at]
            weight = jnp.exp2(parts[at] * (INV_ROOT * LOG2E) - shift)
            total = total + jnp.sum(weight, axis=0, keepdims=True)
            weights.append(weight)
        inverse = 1.0 / total
        for at in range(REACH + 1):
            prob_ref[blocks[at], places[0] : places[0] + TILE] = weights[at] * inverse
        weights = jnp.concatenate(weights, axis=0).astype(BF)
        out_t = dot(val_t, weights, 1, 0) / total
        for j, at in enumerate(places):
            out = out_t[:, j * TOK : (j + 1) * TOK].T.astype(BF)
            out_ref[:, at : at + DIM] = out
            again_ref[:, at : at + DIM] = out

    count = GROUP // heads
    states = {}
    for turn_at in range(count + LAG):
        if turn_at < count:
            states[turn_at] = ready(turn_at * heads)
        if turn_at >= LAG:
            soft(states.pop(turn_at - LAG))


def backward(place_ref, *rest):
    slots = rest[:N_DP]
    shards = rest[N_DP : N_DP + REACH + 1]
    out_ref, prob_ref, query_ref, unit_ref, table_ref = rest[N_DP + REACH + 1 : N_DP + REACH + 6]
    outs = rest[N_DP + REACH + 6 :]
    ds_ref, own_ref = outs[:2]
    part_refs = outs[2 : 2 + REACH]
    gain_ref, rows_ref = outs[2 + REACH :]
    block = place_ref[0, 0]

    @pl.when(pl.program_id(0) == 0)
    def start():
        gain_ref[...] = jnp.zeros_like(gain_ref)

    for slot in range(N_DP):
        rows_ref[slot_rows(slot), :] = slots[slot][...]
    val_b = jnp.concatenate([shards[back][:TOK, DIM:] for back in range(REACH, -1, -1)], axis=0)
    heads = TILE // TOK

    def ready(first):
        places = [(first + j) * DIM for j in range(heads)]
        grads = [rows_ref[:, at : at + DIM] for at in places]
        grad = jnp.concatenate(grads, axis=0)
        deltas = []
        for at, own in zip(places, grads):
            both = own.astype(F32) * out_ref[:, at : at + DIM].astype(F32)
            deltas.append(jnp.sum(both.T, axis=0, keepdims=True))
        return places, grad, jnp.concatenate(deltas, axis=1), dot(val_b, grad, 1, 1)

    def back(state, sums):
        places, grad, delta, dprob = state
        span = slice(places[0], places[0] + TILE)
        probs = prob_ref[:, span]
        dscore = (probs * (dprob - delta)).astype(BF)
        ds_ref[:, span] = dscore
        query = jnp.concatenate([query_ref[:, at : at + DIM] for at in places], axis=0)
        dk = dot(dscore, query, 1, 0)
        dv = dot(probs.astype(BF), grad, 1, 0)
        return (dk, dv) if sums is None else (sums[0] + dk, sums[1] + dv)

    count = GROUP // heads
    states, sums = {}, None
    for turn_at in range(count + LAG):
        if turn_at < count:
            states[turn_at] = ready(turn_at * heads)
        if turn_at >= LAG:
            sums = back(states.pop(turn_at - LAG), sums)
    dk_total, dv_total = sums
    gk_total = jnp.zeros((8, DIM), F32)
    for at, back_by in enumerate(range(REACH, -1, -1)):
        cosine, sine = angles_of(table_ref, jnp.maximum(block - back_by, 0))
        dk_part = dk_total[blocks[at]] * INV_ROOT
        dkn = turn_back(dk_part, cosine, sine)
        gk_total = gk_total + jnp.sum((dkn * unit_ref[blocks[at], :]).reshape(TOK // 8, 8, DIM), axis=0)
        target = own_ref if back_by == 0 else part_refs[back_by - 1]
        target[:, :DIM] = dk_part.astype(target.dtype)
        target[:, DIM:] = dv_total[blocks[at]].astype(target.dtype)
    gain_ref[...] += gk_total


def query_back(place_ref, unit_ref, norm_ref, ds_ref, rot_ref, flip_ref, gq_ref, gk_ref, dq_ref, gain_ref, sum_ref):
    step = pl.program_id(0)

    @pl.when(step == 0)
    def start():
        sum_ref[...] = jnp.zeros_like(sum_ref)

    gain_q = jnp.broadcast_to(gq_ref[...], (TOK, DIM)).T
    cosine, sine = flip_angles(flip_ref, place_ref[0, 0])
    rot_t = rot_ref[...].T
    total = jnp.zeros((DIM, TOK), F32)
    for first in range(0, GROUP * DIM, TILE):
        both = dot(rot_t, ds_ref[:, first : first + TILE], 1, 0) * INV_ROOT
        for at in range(first, first + TILE, TOK):
            dq_t = both[:, at - first : at - first + TOK]
            unit = unit_ref[:, at : at + DIM]
            dqn = dq_t * cosine - half_swap(dq_t) * sine
            total = total + dqn * unit
            scaled = dqn * gain_q
            inner = jnp.mean(scaled * unit, axis=0, keepdims=True)
            back = norm_ref[0:1, at : at + DIM] * (scaled - unit * inner)
            dq_ref[:, at : at + DIM] = back.T.astype(BF)
    sum_ref[...] += total

    @pl.when(step == KV - 1)
    def end():
        spread = (N_DP * N_CP, DIM)
        by_query = jnp.sum(sum_ref[...].T, axis=0, keepdims=True)
        by_key = jnp.sum(gk_ref[...], axis=0, keepdims=True)
        gain_ref[:, :DIM] = jnp.broadcast_to(by_query, spread)
        gain_ref[:, DIM:] = jnp.broadcast_to(by_key, spread)


def finish(place_ref, own_ref, *rest):
    parts = rest[:REACH]
    kv_ref, table_ref, gk_ref, every_ref, dk_ref, dv_ref, gq_out, gk_out = rest[REACH:]
    sums = jnp.sum(every_ref[...], axis=0, keepdims=True) * (1.0 / math.sqrt(TOK * N_DP * N_CP))
    gq_out[...] = sums[:, :DIM]
    gk_out[...] = sums[:, DIM:]
    cosine, sine = angles_of(table_ref, place_ref[0, 0])
    gain_k = gk_ref[...]
    for head in range(KV):
        left = head * PAIR
        both = own_ref[:, left : left + PAIR]
        for part in parts:
            both = both + part[:, left : left + PAIR].astype(F32)
        unit, inv_norm = unit_of(kv_ref[:TOK, left : left + DIM].astype(F32))
        scaled = turn_back(both[:, :DIM], cosine, sine) * gain_k
        inner = jnp.mean(scaled * unit, axis=-1, keepdims=True)
        dk_ref[:, head * DIM : (head + 1) * DIM] = (inv_norm * (scaled - unit * inner)).astype(BF)
        dv_ref[:, head * DIM : (head + 1) * DIM] = both[:, DIM:].astype(BF)


def swap(array, slot):
    return lax.ppermute(array, "dp", [(j, j ^ slot) for j in range(N_DP)])


def shifted(array, by):
    return lax.ppermute(array, "cp", [(j, (j + by) % N_CP) for j in range(N_CP)])


def shape(*dims, dtype=BF):
    return jax.ShapeDtypeStruct(dims, dtype)


def body(q_raw, k_raw, values, loss_grad, send_order, doc_blocks, gain_q, gain_k):
    table_np = tables()
    table = jnp.asarray(table_np)
    flipped = jnp.asarray(np.concatenate([table_np[:, :DIM].T, table_np[:, DIM:].T], axis=1))
    gain_q = gain_q.reshape(1, DIM)
    gain_k = gain_k.reshape(1, DIM)
    kv_slots = pl.pallas_call(
        kv_pick,
        out_shape=[shape(ROWS, KV * PAIR)] * N_DP,
        in_specs=[VMEM] * 3,
        out_specs=[VMEM] * N_DP,
        scratch_shapes=[pltpu.VMEM((TOK, KV * PAIR), BF)],
        compiler_params=pltpu.CompilerParams(vmem_limit_bytes=62 * 1024 * 1024),
        name="kv_pick",
    )(send_order, k_raw, values)
    kv_slots = [kv_slots[0]] + [swap(kv_slots[slot], slot) for slot in range(1, N_DP)]
    half = GROUP * DIM
    picked = pl.pallas_call(
        qg_pick,
        grid=(KV,),
        out_shape=[shape(ROWS, KV * half)] * (2 * N_DP),
        in_specs=[
            pl.BlockSpec((1, TOK), lambda h: (0, 0)),
            pl.BlockSpec((TOK, half), lambda h: (0, h)),
            pl.BlockSpec((TOK, half), lambda h: (0, h)),
        ],
        out_specs=[pl.BlockSpec((ROWS, half), lambda h: (0, h))] * (2 * N_DP),
        scratch_shapes=[pltpu.VMEM((TOK, WIDE), BF)],
        compiler_params=PARAMS,
        name="qg_pick",
    )(send_order, q_raw, loss_grad)
    kv_own = pl.pallas_call(
        kv_join,
        out_shape=shape(TOK + ID_ROWS, KV * PAIR),
        in_specs=[SMEM] + [VMEM] * N_DP,
        out_specs=VMEM,
        compiler_params=PARAMS,
        name="kv_join",
    )(doc_blocks, *kv_slots)
    one = shifted(kv_own, 1)
    two = shifted(kv_own, 2)
    shards = [kv_own, one, two, shifted(one, 2), shifted(two, 2)]
    q_slots = [picked[0]] + [swap(picked[slot], slot) for slot in range(1, N_DP)]
    g_slots = [picked[N_DP]] + [swap(picked[N_DP + slot], slot) for slot in range(1, N_DP)]
    whole = lambda h: (0, 0)
    by_head = lambda h: (0, h)
    slot_specs = [pl.BlockSpec((ROWS, half), by_head)] * N_DP
    shard_specs = [pl.BlockSpec((TOK + ID_ROWS, PAIR), by_head)] * (REACH + 1)
    table_specs = [pl.BlockSpec((KEYS, 2 * DIM), whole)]
    rows_spec = pl.BlockSpec((TOK, half), by_head)
    keys_spec = pl.BlockSpec((KEYS, DIM), by_head)
    square_spec = pl.BlockSpec((KEYS, half), by_head)
    flip_specs = [pl.BlockSpec((DIM, 2 * KEYS), whole)]
    gain_spec = pl.BlockSpec((1, DIM), whole)
    norm_spec = pl.BlockSpec((8, half), by_head)
    part = KEYS // KV
    table_part = pl.BlockSpec((part, 2 * DIM), lambda h: (h, 0))
    flip_part = pl.BlockSpec((DIM // KV, 2 * KEYS), lambda h: (h, 0))
    units, norms, table, flipped = pl.pallas_call(
        query_unit,
        grid=(KV,),
        out_shape=[
            shape(DIM, KV * half, dtype=F32),
            shape(8, KV * half, dtype=F32),
            shape(KEYS, 2 * DIM, dtype=F32),
            shape(DIM, 2 * KEYS, dtype=F32),
        ],
        in_specs=slot_specs + [table_part, flip_part],
        out_specs=[rows_spec, norm_spec, table_part, flip_part],
        scratch_shapes=[pltpu.VMEM((TOK, half), BF)],
        compiler_params=PARAMS,
        name="query_unit",
    )(*q_slots, table, flipped)
    attn_out, out_again, probs, queries, keys_rot, keys_unit, place = pl.pallas_call(
        forward,
        grid=(KV,),
        out_shape=[
            shape(TOK, KV * half),
            shape(TOK, KV * half),
            shape(KEYS, KV * half, dtype=F32),
            shape(TOK, KV * half),
            shape(KEYS, KV * DIM),
            shape(KEYS, KV * DIM, dtype=F32),
            shape(1, 1, dtype=jnp.int32),
        ],
        in_specs=[SMEM, rows_spec] + shard_specs + table_specs + flip_specs + [gain_spec] * 2,
        out_specs=[rows_spec, rows_spec, square_spec, rows_spec, keys_spec, keys_spec, SMEM],
        compiler_params=PARAMS,
        name="forward",
    )(doc_blocks, units, *shards, table, flipped, gain_q, gain_k)
    results = pl.pallas_call(
        backward,
        grid=(KV,),
        out_shape=[shape(KEYS, KV * half), shape(TOK, KV * PAIR, dtype=F32)]
        + [shape(TOK, KV * PAIR)] * REACH
        + [shape(8, DIM, dtype=F32)],
        in_specs=[SMEM]
        + slot_specs
        + shard_specs
        + [rows_spec, square_spec, rows_spec, keys_spec]
        + table_specs,
        out_specs=[square_spec, pl.BlockSpec((TOK, PAIR), by_head)]
        + [pl.BlockSpec((TOK, PAIR), by_head)] * REACH
        + [pl.BlockSpec((8, DIM), whole)],
        scratch_shapes=[pltpu.VMEM((TOK, half), BF)],
        compiler_params=PARAMS,
        name="backward",
    )(place, *g_slots, *shards, out_again, probs, queries, keys_unit, table)
    dscores, dkv_own = results[:2]
    gk_rows = results[2 + REACH]
    parts = [shifted(results[1 + back], -back) for back in range(1, REACH + 1)]

    def query_side(operands):
        place, units, norms, dscores, keys_rot, gk_rows = operands
        dq_raw, gains = pl.pallas_call(
            query_back,
            grid=(KV,),
            out_shape=[shape(TOK, KV * half), shape(N_DP * N_CP, 2 * DIM, dtype=F32)],
            in_specs=[SMEM, rows_spec, norm_spec, square_spec, keys_spec]
            + flip_specs
            + [gain_spec, pl.BlockSpec((8, DIM), whole)],
            out_specs=[rows_spec, pl.BlockSpec((N_DP * N_CP, 2 * DIM), whole)],
            scratch_shapes=[pltpu.VMEM((DIM, TOK), F32)],
            compiler_params=PARAMS,
            name="query_back",
        )(place, units, norms, dscores, keys_rot, flipped, gain_q, gk_rows)
        return dq_raw, lax.all_to_all(gains, ("dp", "cp"), 0, 0, tiled=True)

    def nothing(operands):
        return jnp.zeros((TOK, KV * half), BF), jnp.zeros((N_DP * N_CP, 2 * DIM), F32)

    dq_raw, everyone = lax.cond(
        place[0, 0] >= 0, query_side, nothing, (place, units, norms, dscores, keys_rot, gk_rows)
    )
    dk_raw, dv_out, dgain_q, dgain_k = pl.pallas_call(
        finish,
        out_shape=[shape(TOK, KV * DIM)] * 2 + [shape(1, DIM, dtype=F32)] * 2,
        in_specs=[SMEM] + [VMEM] * (REACH + 5),
        out_specs=[VMEM] * 4,
        compiler_params=PARAMS,
        name="finish",
    )(place, dkv_own, *parts, kv_own, table, gain_k, everyone)
    return attn_out, dq_raw, dk_raw, dv_out, dgain_q.reshape(DIM), dgain_k.reshape(DIM)


def solution(mesh):
    rows = P(("dp", "cp"), None)
    return jax.shard_map(
        body,
        mesh=mesh,
        in_specs=(rows, rows, rows, rows, rows, P("dp", "cp"), P(), P()),
        out_specs=(rows, rows, rows, rows, P(), P()),
        check_vma=False,
    )
```

```python
import math

import jax
import jax.numpy as jnp
import numpy as np
from jax import lax
from jax.experimental import pallas as pl
from jax.experimental.pallas import tpu as pltpu
from jax.sharding import PartitionSpec as P

REACH = 4
EPSILON = 1e-06
THETA = 1000000.0
NEGATIVE = -1e30
TOK = 128
DIM = 128
KV = 4
GROUP = 8
N_DP = 4
N_CP = 64
ROWS = TOK // N_DP
KEYS = (REACH + 1) * TOK
ID_ROWS = 8
TILE = 512
LAG = 1
PAIR = 2 * DIM
WIDE = 2 * GROUP * DIM
HALF = GROUP * DIM
INV_ROOT = 1.0 / math.sqrt(DIM)
LOG2E = 1.4426950408889634
BF = jnp.bfloat16
F32 = jnp.float32
blocks = [slice(at * TOK, (at + 1) * TOK) for at in range(REACH + 1)]
VMEM = pl.BlockSpec(memory_space=pltpu.VMEM)
SMEM = pl.BlockSpec(memory_space=pltpu.SMEM)
VLIM = 24
PARAMS = pltpu.CompilerParams(vmem_limit_bytes=VLIM * 1024 * 1024)


def tables():
    half = DIM // 2
    frequency = (THETA ** (-(np.arange(half) * 2.0 / DIM))).astype(np.float32)
    angles = np.arange(KEYS, dtype=np.float32)[:, None] * frequency[None, :]
    cosine = np.cos(angles.astype(np.float64)).astype(np.float32)
    sine = np.sin(angles.astype(np.float64)).astype(np.float32)
    return np.concatenate([cosine, cosine, -sine, sine], axis=1)


def dot(left, right, left_dim, right_dim):
    return lax.dot_general(
        left, right, (((left_dim,), (right_dim,)), ((), ())), preferred_element_type=F32
    )


def picker(order_ref):
    rows = lax.broadcasted_iota(jnp.int32, (TOK, TOK), 0)
    return jnp.where(rows == order_ref[...], 1.0, 0.0).astype(BF)


def slot_rows(slot):
    place = lax.axis_index("dp") ^ slot
    return pl.ds(pl.multiple_of(place * ROWS, ROWS), ROWS)


def kv_pick(order_ref, k_ref, v_ref, *rest):
    outs, rows_ref = rest[:N_DP], rest[N_DP]
    chosen = picker(order_ref)
    keys = dot(chosen, k_ref[...], 0, 0).astype(BF)
    vals = dot(chosen, v_ref[...], 0, 0).astype(BF)
    for head in range(KV):
        rows_ref[:, head * PAIR : head * PAIR + DIM] = keys[:, head * DIM : (head + 1) * DIM]
        rows_ref[:, head * PAIR + DIM : (head + 1) * PAIR] = vals[:, head * DIM : (head + 1) * DIM]
    for slot in range(N_DP):
        outs[slot][...] = rows_ref[slot_rows(slot), :]


def qg_pick(order_ref, q_ref, g_ref, *rest):
    q_outs, g_outs, rows_ref = rest[:N_DP], rest[N_DP : 2 * N_DP], rest[2 * N_DP]
    chosen = picker(order_ref)
    half = GROUP * DIM
    rows_ref[:, :half] = dot(chosen, q_ref[...], 0, 0).astype(BF)
    rows_ref[:, half:] = dot(chosen, g_ref[...], 0, 0).astype(BF)
    for slot in range(N_DP):
        q_outs[slot][...] = rows_ref[slot_rows(slot), :half]
        g_outs[slot][...] = rows_ref[slot_rows(slot), half:]


def kv_join(doc_ref, *rest):
    slots, out_ref = rest[:N_DP], rest[N_DP]
    for slot in range(N_DP):
        out_ref[slot_rows(slot), :] = slots[slot][...]
    width = out_ref.shape[1]
    out_ref[TOK:, :] = jnp.full((ID_ROWS, width), doc_ref[0, 0], jnp.int32).astype(F32).astype(BF)


def same_docs(doc_ref, shards):
    own = doc_ref[0, 0].astype(F32)
    place = lax.axis_index("cp")
    flags = []
    for back in range(1, REACH + 1):
        near = jnp.max(shards[back][TOK : TOK + ID_ROWS, 0:DIM].astype(F32))
        flags.append(jnp.where((near == own) & (place >= back), 1, 0).astype(jnp.int32))
    return flags


def flip_angles(table_ref, block):
    first = pl.multiple_of(block * TOK, TOK)
    second = pl.multiple_of(block * TOK + KEYS, TOK)
    return table_ref[:, pl.ds(first, TOK)], table_ref[:, pl.ds(second, TOK)]


def columns(head, width, at=0, size=None):
    return pl.ds(pl.multiple_of(head * width + at, DIM), width if size is None else size)


def half_swap(array):
    return jnp.concatenate([array[DIM // 2 :], array[: DIM // 2]], axis=0)


def angles_of(table_ref, block):
    rows = table_ref[pl.ds(pl.multiple_of(block * TOK, TOK), TOK), :]
    return rows[:, :DIM], rows[:, DIM:]


def turn(vectors, cosine, sine):
    return vectors * cosine + pltpu.roll(vectors, DIM // 2, 1) * sine


def turn_back(vectors, cosine, sine):
    return vectors * cosine - pltpu.roll(vectors, DIM // 2, 1) * sine


def unit_of(raw):
    inv_norm = lax.rsqrt(jnp.mean(raw * raw, axis=-1, keepdims=True) + EPSILON)
    return raw * inv_norm, inv_norm


def query_unit(*refs):
    slots = refs[:N_DP]
    table_ref, flip_ref, unit_ref, norm_ref, table_out, flip_out, rows_ref = refs[N_DP:]
    table_out[...] = table_ref[...]
    flip_out[...] = flip_ref[...]
    for slot in range(N_DP):
        rows_ref[slot_rows(slot), :] = slots[slot][...]
    for at in range(0, GROUP * DIM, DIM):
        raw = rows_ref[:, at : at + DIM].astype(F32).T
        inv_norm = lax.rsqrt(jnp.mean(raw * raw, axis=0, keepdims=True) + EPSILON)
        unit_ref[:, at : at + DIM] = raw * inv_norm
        norm_ref[:, at : at + DIM] = jnp.broadcast_to(inv_norm, (8, DIM))


def forward(doc_ref, *rest):
    unitq_ref = rest[0]
    shards = rest[1 : REACH + 2]
    table_ref, flip_ref, gq_ref, gk_ref = rest[REACH + 2 : REACH + 6]
    out_ref, again_ref, prob_ref, query_ref, rot_ref, unit_ref, place_ref = rest[REACH + 6 :]
    flags = same_docs(doc_ref, shards)
    block = flags[0] + flags[1] + flags[2] + flags[3]
    place_ref[0, 0] = block
    gain_q = jnp.broadcast_to(gq_ref[...], (TOK, DIM)).T
    gain_k = gk_ref[...]
    own_cos, own_sin = flip_angles(flip_ref, block)
    levels = [jnp.where(flags[back - 1] > 0, 0.0, NEGATIVE) for back in range(REACH, 0, -1)]
    key = lax.broadcasted_iota(jnp.int32, (TOK, TILE), 0)
    query = lax.broadcasted_iota(jnp.int32, (TOK, TILE), 1) & (TOK - 1)
    causal = key <= query

    @pl.loop(0, KV)
    def each(head):
        key_rot, key_val = [], []
        for at, back in enumerate(range(REACH, -1, -1)):
            cosine, sine = angles_of(table_ref, jnp.maximum(block - back, 0))
            unit, _ = unit_of(shards[back][:TOK, columns(head, PAIR, 0, DIM)].astype(F32))
            turned = turn(unit * gain_k, cosine, sine).astype(BF)
            unit_ref[blocks[at], columns(head, DIM)] = unit
            rot_ref[blocks[at], columns(head, DIM)] = turned
            key_rot.append(turned)
            key_val.append(shards[back][:TOK, columns(head, PAIR, DIM, DIM)])
        rot_f = jnp.concatenate(key_rot, axis=0)
        val_t = jnp.concatenate(key_val, axis=0).T
        heads = TILE // TOK

        def ready(first):
            places = [(first + j) * DIM for j in range(heads)]
            turned = []
            for at in places:
                scaled = unitq_ref[:, columns(head, HALF, at, DIM)] * gain_q
                query_t = scaled * own_cos + half_swap(scaled) * own_sin
                turned.append(query_t.astype(BF))
                query_ref[:, columns(head, HALF, at, DIM)] = query_t.T.astype(BF)
            return places, dot(rot_f, jnp.concatenate(turned, axis=1), 1, 0)

        def soft(state):
            places, scores = state
            last = jnp.where(causal, scores[blocks[REACH]], NEGATIVE)
            parts = [scores[blocks[at]] for at in range(REACH)] + [last]
            tops = [jnp.max(part, axis=0, keepdims=True) for part in parts]
            top = tops[REACH]
            for at in range(REACH):
                top = jnp.maximum(top, tops[at] + levels[at])
            top = top * (INV_ROOT * LOG2E)
            weights, total = [], 0.0
            for at in range(REACH + 1):
                shift = top if at == REACH else top - levels[at]
                weight = jnp.exp2(parts[at] * (INV_ROOT * LOG2E) - shift)
                total = total + jnp.sum(weight, axis=0, keepdims=True)
                weights.append(weight)
            inverse = 1.0 / total
            for at in range(REACH + 1):
                prob_ref[blocks[at], columns(head, HALF, places[0], TILE)] = weights[at] * inverse
            weights = jnp.concatenate(weights, axis=0).astype(BF)
            out_t = dot(val_t, weights, 1, 0) / total
            for j, at in enumerate(places):
                out = out_t[:, j * TOK : (j + 1) * TOK].T.astype(BF)
                out_ref[:, columns(head, HALF, at, DIM)] = out
                again_ref[:, columns(head, HALF, at, DIM)] = out

        count = GROUP // heads
        states = {}
        for turn_at in range(count + LAG):
            if turn_at < count:
                states[turn_at] = ready(turn_at * heads)
            if turn_at >= LAG:
                soft(states.pop(turn_at - LAG))


def backward(place_ref, *rest):
    slots = rest[:N_DP]
    shards = rest[N_DP : N_DP + REACH + 1]
    out_ref, prob_ref, query_ref, unit_ref, table_ref = rest[N_DP + REACH + 1 : N_DP + REACH + 6]
    outs = rest[N_DP + REACH + 6 :]
    ds_ref, own_ref = outs[:2]
    part_refs = outs[2 : 2 + REACH]
    gain_ref, rows_ref = outs[2 + REACH :]
    block = place_ref[0, 0]

    gain_ref[...] = jnp.zeros_like(gain_ref)

    @pl.loop(0, KV)
    def each(head):
        for slot in range(N_DP):
            rows_ref[slot_rows(slot), :] = slots[slot][:, columns(head, HALF)]
        val_b = jnp.concatenate([shards[back][:TOK, columns(head, PAIR, DIM, DIM)] for back in range(REACH, -1, -1)], axis=0)
        heads = TILE // TOK

        def ready(first):
            places = [(first + j) * DIM for j in range(heads)]
            grads = [rows_ref[:, at : at + DIM] for at in places]
            grad = jnp.concatenate(grads, axis=0)
            deltas = []
            for at, own in zip(places, grads):
                both = own.astype(F32) * out_ref[:, columns(head, HALF, at, DIM)].astype(F32)
                deltas.append(jnp.sum(both.T, axis=0, keepdims=True))
            return places, grad, jnp.concatenate(deltas, axis=1), dot(val_b, grad, 1, 1)

        def back(state, sums):
            places, grad, delta, dprob = state
            span = columns(head, HALF, places[0], TILE)
            probs = prob_ref[:, span]
            dscore = (probs * (dprob - delta)).astype(BF)
            ds_ref[:, span] = dscore
            query = jnp.concatenate([query_ref[:, columns(head, HALF, at, DIM)] for at in places], axis=0)
            dk = dot(dscore, query, 1, 0)
            dv = dot(probs.astype(BF), grad, 1, 0)
            return (dk, dv) if sums is None else (sums[0] + dk, sums[1] + dv)

        count = GROUP // heads
        states, sums = {}, None
        for turn_at in range(count + LAG):
            if turn_at < count:
                states[turn_at] = ready(turn_at * heads)
            if turn_at >= LAG:
                sums = back(states.pop(turn_at - LAG), sums)
        dk_total, dv_total = sums
        gk_total = jnp.zeros((8, DIM), F32)
        for at, back_by in enumerate(range(REACH, -1, -1)):
            cosine, sine = angles_of(table_ref, jnp.maximum(block - back_by, 0))
            dk_part = dk_total[blocks[at]] * INV_ROOT
            dkn = turn_back(dk_part, cosine, sine)
            gk_total = gk_total + jnp.sum((dkn * unit_ref[blocks[at], columns(head, DIM)]).reshape(TOK // 8, 8, DIM), axis=0)
            target = own_ref if back_by == 0 else part_refs[back_by - 1]
            target[:, columns(head, PAIR, 0, DIM)] = dk_part.astype(target.dtype)
            target[:, columns(head, PAIR, DIM, DIM)] = dv_total[blocks[at]].astype(target.dtype)
        gain_ref[...] += gk_total


def query_back(place_ref, unit_ref, norm_ref, ds_ref, rot_ref, flip_ref, gq_ref, gk_ref, dq_ref, gain_ref, sum_ref):
    sum_ref[...] = jnp.zeros_like(sum_ref)
    gain_q = jnp.broadcast_to(gq_ref[...], (TOK, DIM)).T
    cosine, sine = flip_angles(flip_ref, place_ref[0, 0])

    @pl.loop(0, KV)
    def each(head):
        rot_t = rot_ref[:, columns(head, DIM)].T
        total = jnp.zeros((DIM, TOK), F32)
        for first in range(0, GROUP * DIM, TILE):
            both = dot(rot_t, ds_ref[:, columns(head, HALF, first, TILE)], 1, 0) * INV_ROOT
            for at in range(first, first + TILE, TOK):
                dq_t = both[:, at - first : at - first + TOK]
                unit = unit_ref[:, columns(head, HALF, at, DIM)]
                dqn = dq_t * cosine - half_swap(dq_t) * sine
                total = total + dqn * unit
                scaled = dqn * gain_q
                inner = jnp.mean(scaled * unit, axis=0, keepdims=True)
                back = norm_ref[0:1, columns(head, HALF, at, DIM)] * (scaled - unit * inner)
                dq_ref[:, columns(head, HALF, at, DIM)] = back.T.astype(BF)
        sum_ref[...] += total

    spread = (8, DIM)
    by_query = jnp.sum(sum_ref[...].T, axis=0, keepdims=True)
    by_key = jnp.sum(gk_ref[...], axis=0, keepdims=True)
    gain_ref[:, :DIM] = jnp.broadcast_to(by_query, spread)
    gain_ref[:, DIM:] = jnp.broadcast_to(by_key, spread)


def finish(place_ref, own_ref, *rest):
    parts = rest[:REACH]
    kv_ref, table_ref, gk_ref, every_ref, dk_ref, dv_ref, gq_out, gk_out = rest[REACH:]
    sums = jnp.sum(every_ref[...], axis=0, keepdims=True) * (1.0 / math.sqrt(TOK * N_DP * N_CP))
    gq_out[...] = sums[:, :DIM]
    gk_out[...] = sums[:, DIM:]
    cosine, sine = angles_of(table_ref, place_ref[0, 0])
    gain_k = gk_ref[...]
    for head in range(KV):
        left = head * PAIR
        both = own_ref[:, left : left + PAIR]
        for part in parts:
            both = both + part[:, left : left + PAIR].astype(F32)
        unit, inv_norm = unit_of(kv_ref[:TOK, left : left + DIM].astype(F32))
        scaled = turn_back(both[:, :DIM], cosine, sine) * gain_k
        inner = jnp.mean(scaled * unit, axis=-1, keepdims=True)
        dk_ref[:, head * DIM : (head + 1) * DIM] = (inv_norm * (scaled - unit * inner)).astype(BF)
        dv_ref[:, head * DIM : (head + 1) * DIM] = both[:, DIM:].astype(BF)


def swap(array, slot):
    return lax.ppermute(array, "dp", [(j, j ^ slot) for j in range(N_DP)])


def shifted(array, by):
    return lax.ppermute(array, "cp", [(j, (j + by) % N_CP) for j in range(N_CP)])


def shape(*dims, dtype=BF):
    return jax.ShapeDtypeStruct(dims, dtype)


def body(q_raw, k_raw, values, loss_grad, send_order, doc_blocks, gain_q, gain_k):
    table_np = tables()
    table = jnp.asarray(table_np)
    flipped = jnp.asarray(np.concatenate([table_np[:, :DIM].T, table_np[:, DIM:].T], axis=1))
    gain_q = gain_q.reshape(1, DIM)
    gain_k = gain_k.reshape(1, DIM)
    kv_slots = pl.pallas_call(
        kv_pick,
        out_shape=[shape(ROWS, KV * PAIR)] * N_DP,
        in_specs=[VMEM] * 3,
        out_specs=[VMEM] * N_DP,
        scratch_shapes=[pltpu.VMEM((TOK, KV * PAIR), BF)],
        compiler_params=pltpu.CompilerParams(vmem_limit_bytes=62 * 1024 * 1024),
        name="kv_pick",
    )(send_order, k_raw, values)
    kv_slots = [kv_slots[0]] + [swap(kv_slots[slot], slot) for slot in range(1, N_DP)]
    half = GROUP * DIM
    picked = pl.pallas_call(
        qg_pick,
        grid=(KV,),
        out_shape=[shape(ROWS, KV * half)] * (2 * N_DP),
        in_specs=[
            pl.BlockSpec((1, TOK), lambda h: (0, 0)),
            pl.BlockSpec((TOK, half), lambda h: (0, h)),
            pl.BlockSpec((TOK, half), lambda h: (0, h)),
        ],
        out_specs=[pl.BlockSpec((ROWS, half), lambda h: (0, h))] * (2 * N_DP),
        scratch_shapes=[pltpu.VMEM((TOK, WIDE), BF)],
        compiler_params=PARAMS,
        name="qg_pick",
    )(send_order, q_raw, loss_grad)
    kv_own = pl.pallas_call(
        kv_join,
        out_shape=shape(TOK + ID_ROWS, KV * PAIR),
        in_specs=[SMEM] + [VMEM] * N_DP,
        out_specs=VMEM,
        compiler_params=PARAMS,
        name="kv_join",
    )(doc_blocks, *kv_slots)
    one = shifted(kv_own, 1)
    shards = [kv_own, one, shifted(kv_own, 2), shifted(one, 2), shifted(kv_own, 4)]
    q_slots = [picked[0]] + [swap(picked[slot], slot) for slot in range(1, N_DP)]
    g_slots = [picked[N_DP]] + [swap(picked[N_DP + slot], slot) for slot in range(1, N_DP)]
    whole = lambda h: (0, 0)
    by_head = lambda h: (0, h)
    slot_specs = [pl.BlockSpec((ROWS, half), by_head)] * N_DP
    shard_specs = [pl.BlockSpec((TOK + ID_ROWS, PAIR), by_head)] * (REACH + 1)
    table_specs = [pl.BlockSpec((KEYS, 2 * DIM), whole)]
    rows_spec = pl.BlockSpec((TOK, half), by_head)
    keys_spec = pl.BlockSpec((KEYS, DIM), by_head)
    square_spec = pl.BlockSpec((KEYS, half), by_head)
    flip_specs = [pl.BlockSpec((DIM, 2 * KEYS), whole)]
    gain_spec = pl.BlockSpec((1, DIM), whole)
    norm_spec = pl.BlockSpec((8, half), by_head)
    part = KEYS // KV
    table_part = pl.BlockSpec((part, 2 * DIM), lambda h: (h, 0))
    flip_part = pl.BlockSpec((DIM // KV, 2 * KEYS), lambda h: (h, 0))
    units, norms, table, flipped = pl.pallas_call(
        query_unit,
        grid=(KV,),
        out_shape=[
            shape(DIM, KV * half, dtype=F32),
            shape(8, KV * half, dtype=F32),
            shape(KEYS, 2 * DIM, dtype=F32),
            shape(DIM, 2 * KEYS, dtype=F32),
        ],
        in_specs=slot_specs + [table_part, flip_part],
        out_specs=[rows_spec, norm_spec, table_part, flip_part],
        scratch_shapes=[pltpu.VMEM((TOK, half), BF)],
        compiler_params=PARAMS,
        name="query_unit",
    )(*q_slots, table, flipped)
    attn_out, out_again, probs, queries, keys_rot, keys_unit, place = pl.pallas_call(
        forward,
        out_shape=[
            shape(TOK, KV * half),
            shape(TOK, KV * half),
            shape(KEYS, KV * half, dtype=F32),
            shape(TOK, KV * half),
            shape(KEYS, KV * DIM),
            shape(KEYS, KV * DIM, dtype=F32),
            shape(1, 1, dtype=jnp.int32),
        ],
        in_specs=[SMEM] + [VMEM] * (REACH + 6),
        out_specs=[VMEM] * 6 + [SMEM],
        compiler_params=PARAMS,
        name="forward",
    )(doc_blocks, units, *shards, table, flipped, gain_q, gain_k)
    results = pl.pallas_call(
        backward,
        out_shape=[shape(KEYS, KV * half), shape(TOK, KV * PAIR, dtype=F32)]
        + [shape(TOK, KV * PAIR)] * REACH
        + [shape(8, DIM, dtype=F32)],
        in_specs=[SMEM] + [VMEM] * (N_DP + REACH + 6),
        out_specs=[VMEM] * (3 + REACH),
        scratch_shapes=[pltpu.VMEM((TOK, half), BF)],
        compiler_params=PARAMS,
        name="backward",
    )(place, *g_slots, *shards, out_again, probs, queries, keys_unit, table)
    dscores, dkv_own = results[:2]
    gk_rows = results[2 + REACH]
    parts = [shifted(results[1 + back], -back) for back in range(1, REACH + 1)]

    def query_side(operands):
        place, units, norms, dscores, keys_rot, gk_rows = operands
        dq_raw, gains = pl.pallas_call(
            query_back,
            out_shape=[shape(TOK, KV * half), shape(8, 2 * DIM, dtype=F32)],
            in_specs=[SMEM] + [VMEM] * 7,
            out_specs=[VMEM] * 2,
            scratch_shapes=[pltpu.VMEM((DIM, TOK), F32)],
            compiler_params=PARAMS,
            name="query_back",
        )(place, units, norms, dscores, keys_rot, flipped, gain_q, gk_rows)
        gains = gains[0:1] + swap(gains, 1)[0:1]
        gains = jnp.broadcast_to(gains, (2 * N_CP, 2 * DIM))
        groups = [
            [(2 * chip + core) * N_CP + place for chip in range(2) for place in range(N_CP)]
            for core in range(2)
        ]
        return dq_raw, lax.all_to_all(
            gains, ("dp", "cp"), 0, 0, tiled=True, axis_index_groups=groups
        )

    def nothing(operands):
        return jnp.zeros((TOK, KV * half), BF), jnp.zeros((2 * N_CP, 2 * DIM), F32)

    dq_raw, everyone = lax.cond(
        place[0, 0] >= 0, query_side, nothing, (place, units, norms, dscores, keys_rot, gk_rows)
    )
    dk_raw, dv_out, dgain_q, dgain_k = pl.pallas_call(
        finish,
        out_shape=[shape(TOK, KV * DIM)] * 2 + [shape(1, DIM, dtype=F32)] * 2,
        in_specs=[SMEM] + [VMEM] * (REACH + 5),
        out_specs=[VMEM] * 4,
        compiler_params=PARAMS,
        name="finish",
    )(place, dkv_own, *parts, kv_own, table, gain_k, everyone)
    return attn_out, dq_raw, dk_raw, dv_out, dgain_q.reshape(DIM), dgain_k.reshape(DIM)


def solution(mesh):
    rows = P(("dp", "cp"), None)
    return jax.shard_map(
        body,
        mesh=mesh,
        in_specs=(rows, rows, rows, rows, rows, P("dp", "cp"), P(), P()),
        out_specs=(rows, rows, rows, rows, P(), P()),
        check_vma=False,
    )
```

```python
import math

import jax
import jax.numpy as jnp
import numpy as np
from jax import lax
from jax.experimental import pallas as pl
from jax.experimental.pallas import tpu as pltpu
from jax.sharding import PartitionSpec as P

REACH = 4
EPSILON = 1e-06
THETA = 1000000.0
NEGATIVE = -1e30
TOK = 128
DIM = 128
KV = 4
GROUP = 8
N_DP = 4
N_CP = 64
ROWS = TOK // N_DP
KEYS = (REACH + 1) * TOK
ID_ROWS = 8
TILE = 512
LAG = 1
PAIR = 2 * DIM
WIDE = 2 * GROUP * DIM
HALF = GROUP * DIM
INV_ROOT = 1.0 / math.sqrt(DIM)
LOG2E = 1.4426950408889634
BF = jnp.bfloat16
F32 = jnp.float32
blocks = [slice(at * TOK, (at + 1) * TOK) for at in range(REACH + 1)]
VMEM = pl.BlockSpec(memory_space=pltpu.VMEM)
SMEM = pl.BlockSpec(memory_space=pltpu.SMEM)
VLIM = 24
PARAMS = pltpu.CompilerParams(vmem_limit_bytes=VLIM * 1024 * 1024)


def tables():
    half = DIM // 2
    frequency = (THETA ** (-(np.arange(half) * 2.0 / DIM))).astype(np.float32)
    angles = np.arange(KEYS, dtype=np.float32)[:, None] * frequency[None, :]
    cosine = np.cos(angles.astype(np.float64)).astype(np.float32)
    sine = np.sin(angles.astype(np.float64)).astype(np.float32)
    return np.concatenate([cosine, cosine, -sine, sine], axis=1)


def dot(left, right, left_dim, right_dim):
    return lax.dot_general(
        left, right, (((left_dim,), (right_dim,)), ((), ())), preferred_element_type=F32
    )


def picker(order_ref):
    rows = lax.broadcasted_iota(jnp.int32, (TOK, TOK), 0)
    return jnp.where(rows == order_ref[...], 1.0, 0.0).astype(BF)


def slot_rows(slot):
    place = lax.axis_index("dp") ^ slot
    return pl.ds(pl.multiple_of(place * ROWS, ROWS), ROWS)


def kv_pick(order_ref, k_ref, v_ref, *rest):
    outs, rows_ref = rest[:N_DP], rest[N_DP]
    chosen = picker(order_ref)
    keys = dot(chosen, k_ref[...], 0, 0).astype(BF)
    vals = dot(chosen, v_ref[...], 0, 0).astype(BF)
    for head in range(KV):
        rows_ref[:, head * PAIR : head * PAIR + DIM] = keys[:, head * DIM : (head + 1) * DIM]
        rows_ref[:, head * PAIR + DIM : (head + 1) * PAIR] = vals[:, head * DIM : (head + 1) * DIM]
    for slot in range(N_DP):
        outs[slot][...] = rows_ref[slot_rows(slot), :]


def qg_pick(order_ref, q_ref, g_ref, *rest):
    q_outs, g_outs, rows_ref = rest[:N_DP], rest[N_DP : 2 * N_DP], rest[2 * N_DP]
    chosen = picker(order_ref)
    half = GROUP * DIM
    rows_ref[:, :half] = dot(chosen, q_ref[...], 0, 0).astype(BF)
    rows_ref[:, half:] = dot(chosen, g_ref[...], 0, 0).astype(BF)
    for slot in range(N_DP):
        q_outs[slot][...] = rows_ref[slot_rows(slot), :half]
        g_outs[slot][...] = rows_ref[slot_rows(slot), half:]


def kv_join(doc_ref, *rest):
    slots, out_ref = rest[:N_DP], rest[N_DP]
    for slot in range(N_DP):
        out_ref[slot_rows(slot), :] = slots[slot][...]
    width = out_ref.shape[1]
    out_ref[TOK:, :] = jnp.full((ID_ROWS, width), doc_ref[0, 0], jnp.int32).astype(F32).astype(BF)


def same_docs(doc_ref, shards):
    own = doc_ref[0, 0].astype(F32)
    place = lax.axis_index("cp")
    flags = []
    for back in range(1, REACH + 1):
        near = jnp.max(shards[back][TOK : TOK + ID_ROWS, 0:DIM].astype(F32))
        flags.append(jnp.where((near == own) & (place >= back), 1, 0).astype(jnp.int32))
    return flags


def flip_angles(table_ref, block):
    first = pl.multiple_of(block * TOK, TOK)
    second = pl.multiple_of(block * TOK + KEYS, TOK)
    return table_ref[:, pl.ds(first, TOK)], table_ref[:, pl.ds(second, TOK)]


def columns(head, width, at=0, size=None):
    return pl.ds(pl.multiple_of(head * width + at, DIM), width if size is None else size)


def half_swap(array):
    return jnp.concatenate([array[DIM // 2 :], array[: DIM // 2]], axis=0)


def angles_of(table_ref, block):
    rows = table_ref[pl.ds(pl.multiple_of(block * TOK, TOK), TOK), :]
    return rows[:, :DIM], rows[:, DIM:]


def turn(vectors, cosine, sine):
    return vectors * cosine + pltpu.roll(vectors, DIM // 2, 1) * sine


def turn_back(vectors, cosine, sine):
    return vectors * cosine - pltpu.roll(vectors, DIM // 2, 1) * sine


def unit_of(raw):
    inv_norm = lax.rsqrt(jnp.mean(raw * raw, axis=-1, keepdims=True) + EPSILON)
    return raw * inv_norm, inv_norm


def query_unit(*refs):
    slots = refs[:N_DP]
    table_ref, flip_ref, unit_ref, norm_ref, table_out, flip_out, rows_ref = refs[N_DP:]
    table_out[...] = table_ref[...]
    flip_out[...] = flip_ref[...]
    for slot in range(N_DP):
        rows_ref[slot_rows(slot), :] = slots[slot][...]
    for at in range(0, GROUP * DIM, DIM):
        raw = rows_ref[:, at : at + DIM].astype(F32).T
        inv_norm = lax.rsqrt(jnp.mean(raw * raw, axis=0, keepdims=True) + EPSILON)
        unit_ref[:, at : at + DIM] = raw * inv_norm
        norm_ref[:, at : at + DIM] = jnp.broadcast_to(inv_norm, (8, DIM))


def forward(doc_ref, *rest):
    unitq_ref = rest[0]
    shards = rest[1 : REACH + 2]
    table_ref, flip_ref, gq_ref, gk_ref = rest[REACH + 2 : REACH + 6]
    out_ref, again_ref, prob_ref, query_ref, rot_ref, unit_ref, place_ref = rest[REACH + 6 :]
    flags = same_docs(doc_ref, shards)
    block = flags[0] + flags[1] + flags[2] + flags[3]
    place_ref[0, 0] = block
    gain_q = jnp.broadcast_to(gq_ref[...], (TOK, DIM)).T
    gain_k = gk_ref[...]
    own_cos, own_sin = flip_angles(flip_ref, block)
    levels = [jnp.where(flags[back - 1] > 0, 0.0, NEGATIVE) for back in range(REACH, 0, -1)]
    key = lax.broadcasted_iota(jnp.int32, (TOK, TILE), 0)
    query = lax.broadcasted_iota(jnp.int32, (TOK, TILE), 1) & (TOK - 1)
    causal = key <= query

    @pl.loop(0, KV)
    def each(head):
        key_rot, key_val = [], []
        for at, back in enumerate(range(REACH, -1, -1)):
            cosine, sine = angles_of(table_ref, jnp.maximum(block - back, 0))
            unit, _ = unit_of(shards[back][:TOK, columns(head, PAIR, 0, DIM)].astype(F32))
            turned = turn(unit * gain_k, cosine, sine).astype(BF)
            unit_ref[blocks[at], columns(head, DIM)] = unit
            rot_ref[blocks[at], columns(head, DIM)] = turned
            key_rot.append(turned)
            key_val.append(shards[back][:TOK, columns(head, PAIR, DIM, DIM)])
        rot_f = jnp.concatenate(key_rot, axis=0)
        val_t = jnp.concatenate(key_val, axis=0).T
        heads = TILE // TOK

        def ready(first):
            places = [(first + j) * DIM for j in range(heads)]
            turned = []
            for at in places:
                scaled = unitq_ref[:, columns(head, HALF, at, DIM)] * gain_q
                query_t = scaled * own_cos + half_swap(scaled) * own_sin
                turned.append(query_t.astype(BF))
                query_ref[:, columns(head, HALF, at, DIM)] = query_t.T.astype(BF)
            return places, dot(rot_f, jnp.concatenate(turned, axis=1), 1, 0)

        def soft(state):
            places, scores = state
            last = jnp.where(causal, scores[blocks[REACH]], NEGATIVE)
            parts = [scores[blocks[at]] for at in range(REACH)] + [last]
            tops = [jnp.max(part, axis=0, keepdims=True) for part in parts]
            top = tops[REACH]
            for at in range(REACH):
                top = jnp.maximum(top, tops[at] + levels[at])
            top = top * (INV_ROOT * LOG2E)
            weights, total = [], 0.0
            for at in range(REACH + 1):
                shift = top if at == REACH else top - levels[at]
                weight = jnp.exp2(parts[at] * (INV_ROOT * LOG2E) - shift)
                total = total + jnp.sum(weight, axis=0, keepdims=True)
                weights.append(weight)
            inverse = 1.0 / total
            for at in range(REACH + 1):
                prob_ref[blocks[at], columns(head, HALF, places[0], TILE)] = weights[at] * inverse
            weights = jnp.concatenate(weights, axis=0).astype(BF)
            out_t = dot(val_t, weights, 1, 0) / total
            for j, at in enumerate(places):
                out = out_t[:, j * TOK : (j + 1) * TOK].T.astype(BF)
                out_ref[:, columns(head, HALF, at, DIM)] = out
                again_ref[:, columns(head, HALF, at, DIM)] = out

        count = GROUP // heads
        states = {}
        for turn_at in range(count + LAG):
            if turn_at < count:
                states[turn_at] = ready(turn_at * heads)
            if turn_at >= LAG:
                soft(states.pop(turn_at - LAG))


def backward(place_ref, *rest):
    slots = rest[:N_DP]
    shards = rest[N_DP : N_DP + REACH + 1]
    out_ref, prob_ref, query_ref, unit_ref, table_ref = rest[N_DP + REACH + 1 : N_DP + REACH + 6]
    outs = rest[N_DP + REACH + 6 :]
    ds_ref, own_ref = outs[:2]
    part_refs = outs[2 : 2 + REACH]
    gain_ref, rows_ref = outs[2 + REACH :]
    block = place_ref[0, 0]

    gain_ref[...] = jnp.zeros_like(gain_ref)

    @pl.loop(0, KV)
    def each(head):
        for slot in range(N_DP):
            rows_ref[slot_rows(slot), :] = slots[slot][:, columns(head, HALF)]
        val_b = jnp.concatenate([shards[back][:TOK, columns(head, PAIR, DIM, DIM)] for back in range(REACH, -1, -1)], axis=0)
        heads = TILE // TOK

        def ready(first):
            places = [(first + j) * DIM for j in range(heads)]
            grads = [rows_ref[:, at : at + DIM] for at in places]
            grad = jnp.concatenate(grads, axis=0)
            deltas = []
            for at, own in zip(places, grads):
                both = own.astype(F32) * out_ref[:, columns(head, HALF, at, DIM)].astype(F32)
                deltas.append(jnp.sum(both.T, axis=0, keepdims=True))
            return places, grad, jnp.concatenate(deltas, axis=1), dot(val_b, grad, 1, 1)

        def back(state, sums):
            places, grad, delta, dprob = state
            span = columns(head, HALF, places[0], TILE)
            probs = prob_ref[:, span]
            dscore = (probs * (dprob - delta)).astype(BF)
            ds_ref[:, span] = dscore
            query = jnp.concatenate([query_ref[:, columns(head, HALF, at, DIM)] for at in places], axis=0)
            dk = dot(dscore, query, 1, 0)
            dv = dot(probs.astype(BF), grad, 1, 0)
            return (dk, dv) if sums is None else (sums[0] + dk, sums[1] + dv)

        count = GROUP // heads
        states, sums = {}, None
        for turn_at in range(count + LAG):
            if turn_at < count:
                states[turn_at] = ready(turn_at * heads)
            if turn_at >= LAG:
                sums = back(states.pop(turn_at - LAG), sums)
        dk_total, dv_total = sums
        gk_total = jnp.zeros((8, DIM), F32)
        for at, back_by in enumerate(range(REACH, -1, -1)):
            cosine, sine = angles_of(table_ref, jnp.maximum(block - back_by, 0))
            dk_part = dk_total[blocks[at]] * INV_ROOT
            dkn = turn_back(dk_part, cosine, sine)
            gk_total = gk_total + jnp.sum((dkn * unit_ref[blocks[at], columns(head, DIM)]).reshape(TOK // 8, 8, DIM), axis=0)
            target = own_ref if back_by == 0 else part_refs[back_by - 1]
            target[:, columns(head, PAIR, 0, DIM)] = dk_part.astype(target.dtype)
            target[:, columns(head, PAIR, DIM, DIM)] = dv_total[blocks[at]].astype(target.dtype)
        gain_ref[...] += gk_total


def query_back(place_ref, unit_ref, norm_ref, ds_ref, rot_ref, flip_ref, gq_ref, gk_ref, dq_ref, gain_ref, sum_ref):
    sum_ref[...] = jnp.zeros_like(sum_ref)
    gain_q = jnp.broadcast_to(gq_ref[...], (TOK, DIM)).T
    cosine, sine = flip_angles(flip_ref, place_ref[0, 0])

    @pl.loop(0, KV)
    def each(head):
        rot_t = rot_ref[:, columns(head, DIM)].T
        total = jnp.zeros((DIM, TOK), F32)
        for first in range(0, GROUP * DIM, TILE):
            both = dot(rot_t, ds_ref[:, columns(head, HALF, first, TILE)], 1, 0) * INV_ROOT
            for at in range(first, first + TILE, TOK):
                dq_t = both[:, at - first : at - first + TOK]
                unit = unit_ref[:, columns(head, HALF, at, DIM)]
                dqn = dq_t * cosine - half_swap(dq_t) * sine
                total = total + dqn * unit
                scaled = dqn * gain_q
                inner = jnp.mean(scaled * unit, axis=0, keepdims=True)
                back = norm_ref[0:1, columns(head, HALF, at, DIM)] * (scaled - unit * inner)
                dq_ref[:, columns(head, HALF, at, DIM)] = back.T.astype(BF)
        sum_ref[...] += total

    spread = (8, DIM)
    by_query = jnp.sum(sum_ref[...].T, axis=0, keepdims=True)
    by_key = jnp.sum(gk_ref[...], axis=0, keepdims=True)
    gain_ref[:, :DIM] = jnp.broadcast_to(by_query, spread)
    gain_ref[:, DIM:] = jnp.broadcast_to(by_key, spread)


def finish(place_ref, own_ref, *rest):
    parts = rest[:REACH]
    kv_ref, table_ref, gk_ref, every_ref, dk_ref, dv_ref, gq_out, gk_out = rest[REACH:]
    sums = jnp.sum(every_ref[...], axis=0, keepdims=True) * (1.0 / math.sqrt(TOK * N_DP * N_CP))
    gq_out[...] = sums[:, :DIM]
    gk_out[...] = sums[:, DIM:]
    cosine, sine = angles_of(table_ref, place_ref[0, 0])
    gain_k = gk_ref[...]
    for head in range(KV):
        left = head * PAIR
        both = own_ref[:, left : left + PAIR]
        for part in parts:
            both = both + part[:, left : left + PAIR].astype(F32)
        unit, inv_norm = unit_of(kv_ref[:TOK, left : left + DIM].astype(F32))
        scaled = turn_back(both[:, :DIM], cosine, sine) * gain_k
        inner = jnp.mean(scaled * unit, axis=-1, keepdims=True)
        dk_ref[:, head * DIM : (head + 1) * DIM] = (inv_norm * (scaled - unit * inner)).astype(BF)
        dv_ref[:, head * DIM : (head + 1) * DIM] = both[:, DIM:].astype(BF)


def swap(array, slot):
    return lax.ppermute(array, "dp", [(j, j ^ slot) for j in range(N_DP)])


def shifted(array, by):
    return lax.ppermute(array, "cp", [(j, (j + by) % N_CP) for j in range(N_CP)])


def shape(*dims, dtype=BF):
    return jax.ShapeDtypeStruct(dims, dtype)


def body(q_raw, k_raw, values, loss_grad, send_order, doc_blocks, gain_q, gain_k):
    table_np = tables()
    table = jnp.asarray(table_np)
    flipped = jnp.asarray(np.concatenate([table_np[:, :DIM].T, table_np[:, DIM:].T], axis=1))
    gain_q = gain_q.reshape(1, DIM)
    gain_k = gain_k.reshape(1, DIM)
    kv_slots = pl.pallas_call(
        kv_pick,
        out_shape=[shape(ROWS, KV * PAIR)] * N_DP,
        in_specs=[VMEM] * 3,
        out_specs=[VMEM] * N_DP,
        scratch_shapes=[pltpu.VMEM((TOK, KV * PAIR), BF)],
        compiler_params=pltpu.CompilerParams(vmem_limit_bytes=62 * 1024 * 1024),
        name="kv_pick",
    )(send_order, k_raw, values)
    kv_slots = [kv_slots[0]] + [swap(kv_slots[slot], slot) for slot in range(1, N_DP)]
    half = GROUP * DIM
    picked = pl.pallas_call(
        qg_pick,
        grid=(KV,),
        out_shape=[shape(ROWS, KV * half)] * (2 * N_DP),
        in_specs=[
            pl.BlockSpec((1, TOK), lambda h: (0, 0)),
            pl.BlockSpec((TOK, half), lambda h: (0, h)),
            pl.BlockSpec((TOK, half), lambda h: (0, h)),
        ],
        out_specs=[pl.BlockSpec((ROWS, half), lambda h: (0, h))] * (2 * N_DP),
        scratch_shapes=[pltpu.VMEM((TOK, WIDE), BF)],
        compiler_params=PARAMS,
        name="qg_pick",
    )(send_order, q_raw, loss_grad)
    kv_own = pl.pallas_call(
        kv_join,
        out_shape=shape(TOK + ID_ROWS, KV * PAIR),
        in_specs=[SMEM] + [VMEM] * N_DP,
        out_specs=VMEM,
        compiler_params=PARAMS,
        name="kv_join",
    )(doc_blocks, *kv_slots)
    one = shifted(kv_own, 1)
    shards = [kv_own, one, shifted(kv_own, 2), shifted(one, 2), shifted(kv_own, 4)]
    q_slots = [picked[0]] + [swap(picked[slot], slot) for slot in range(1, N_DP)]
    g_slots = [picked[N_DP]] + [swap(picked[N_DP + slot], slot) for slot in range(1, N_DP)]
    whole = lambda h: (0, 0)
    by_head = lambda h: (0, h)
    slot_specs = [pl.BlockSpec((ROWS, half), by_head)] * N_DP
    shard_specs = [pl.BlockSpec((TOK + ID_ROWS, PAIR), by_head)] * (REACH + 1)
    table_specs = [pl.BlockSpec((KEYS, 2 * DIM), whole)]
    rows_spec = pl.BlockSpec((TOK, half), by_head)
    keys_spec = pl.BlockSpec((KEYS, DIM), by_head)
    square_spec = pl.BlockSpec((KEYS, half), by_head)
    flip_specs = [pl.BlockSpec((DIM, 2 * KEYS), whole)]
    gain_spec = pl.BlockSpec((1, DIM), whole)
    norm_spec = pl.BlockSpec((8, half), by_head)
    part = KEYS // KV
    table_part = pl.BlockSpec((part, 2 * DIM), lambda h: (h, 0))
    flip_part = pl.BlockSpec((DIM // KV, 2 * KEYS), lambda h: (h, 0))
    units, norms, table, flipped = pl.pallas_call(
        query_unit,
        grid=(KV,),
        out_shape=[
            shape(DIM, KV * half, dtype=F32),
            shape(8, KV * half, dtype=F32),
            shape(KEYS, 2 * DIM, dtype=F32),
            shape(DIM, 2 * KEYS, dtype=F32),
        ],
        in_specs=slot_specs + [table_part, flip_part],
        out_specs=[rows_spec, norm_spec, table_part, flip_part],
        scratch_shapes=[pltpu.VMEM((TOK, half), BF)],
        compiler_params=PARAMS,
        name="query_unit",
    )(*q_slots, table, flipped)
    attn_out, out_again, probs, queries, keys_rot, keys_unit, place = pl.pallas_call(
        forward,
        out_shape=[
            shape(TOK, KV * half),
            shape(TOK, KV * half),
            shape(KEYS, KV * half, dtype=F32),
            shape(TOK, KV * half),
            shape(KEYS, KV * DIM),
            shape(KEYS, KV * DIM, dtype=F32),
            shape(1, 1, dtype=jnp.int32),
        ],
        in_specs=[SMEM] + [VMEM] * (REACH + 6),
        out_specs=[VMEM] * 6 + [SMEM],
        compiler_params=PARAMS,
        name="forward",
    )(doc_blocks, units, *shards, table, flipped, gain_q, gain_k)
    results = pl.pallas_call(
        backward,
        out_shape=[shape(KEYS, KV * half), shape(TOK, KV * PAIR, dtype=F32)]
        + [shape(TOK, KV * PAIR)] * REACH
        + [shape(8, DIM, dtype=F32)],
        in_specs=[SMEM] + [VMEM] * (N_DP + REACH + 6),
        out_specs=[VMEM] * (3 + REACH),
        scratch_shapes=[pltpu.VMEM((TOK, half), BF)],
        compiler_params=PARAMS,
        name="backward",
    )(place, *g_slots, *shards, out_again, probs, queries, keys_unit, table)
    dscores, dkv_own = results[:2]
    gk_rows = results[2 + REACH]
    parts = [shifted(results[1 + back], -back) for back in (4, 2, 3, 1)]

    def query_side(operands):
        place, units, norms, dscores, keys_rot, gk_rows = operands
        dq_raw, gains = pl.pallas_call(
            query_back,
            out_shape=[shape(TOK, KV * half), shape(8, 2 * DIM, dtype=F32)],
            in_specs=[SMEM] + [VMEM] * 7,
            out_specs=[VMEM] * 2,
            scratch_shapes=[pltpu.VMEM((DIM, TOK), F32)],
            compiler_params=PARAMS,
            name="query_back",
        )(place, units, norms, dscores, keys_rot, flipped, gain_q, gk_rows)
        gains = gains[0:1] + swap(gains, 1)[0:1]
        gains = jnp.broadcast_to(gains, (2 * N_CP, 2 * DIM))
        groups = [
            [(2 * chip + core) * N_CP + place for chip in range(2) for place in range(N_CP)]
            for core in range(2)
        ]
        return dq_raw, lax.all_to_all(
            gains, ("dp", "cp"), 0, 0, tiled=True, axis_index_groups=groups
        )

    def nothing(operands):
        return jnp.zeros((TOK, KV * half), BF), jnp.zeros((2 * N_CP, 2 * DIM), F32)

    dq_raw, everyone = lax.cond(
        place[0, 0] >= 0, query_side, nothing, (place, units, norms, dscores, keys_rot, gk_rows)
    )
    dk_raw, dv_out, dgain_q, dgain_k = pl.pallas_call(
        finish,
        out_shape=[shape(TOK, KV * DIM)] * 2 + [shape(1, DIM, dtype=F32)] * 2,
        in_specs=[SMEM] + [VMEM] * (REACH + 5),
        out_specs=[VMEM] * 4,
        compiler_params=PARAMS,
        name="finish",
    )(place, dkv_own, *parts, kv_own, table, gain_k, everyone)
    return attn_out, dq_raw, dk_raw, dv_out, dgain_q.reshape(DIM), dgain_k.reshape(DIM)


def solution(mesh):
    rows = P(("dp", "cp"), None)
    return jax.shard_map(
        body,
        mesh=mesh,
        in_specs=(rows, rows, rows, rows, rows, P("dp", "cp"), P(), P()),
        out_specs=(rows, rows, rows, rows, P(), P()),
        check_vma=False,
    )
```

```python
import math

import jax
import jax.numpy as jnp
import numpy as np
from jax import lax
from jax.experimental import pallas as pl
from jax.experimental.pallas import tpu as pltpu
from jax.sharding import PartitionSpec as P

REACH = 4
EPSILON = 1e-06
THETA = 1000000.0
NEGATIVE = -1e30
TOK = 128
DIM = 128
KV = 4
GROUP = 8
N_DP = 4
N_CP = 64
ROWS = TOK // N_DP
KEYS = (REACH + 1) * TOK
ID_ROWS = 8
TILE = 512
LAG = 1
PAIR = 2 * DIM
WIDE = 2 * GROUP * DIM
HALF = GROUP * DIM
INV_ROOT = 1.0 / math.sqrt(DIM)
LOG2E = 1.4426950408889634
BF = jnp.bfloat16
F32 = jnp.float32
blocks = [slice(at * TOK, (at + 1) * TOK) for at in range(REACH + 1)]
VMEM = pl.BlockSpec(memory_space=pltpu.VMEM)
SMEM = pl.BlockSpec(memory_space=pltpu.SMEM)
VLIM = 24
PARAMS = pltpu.CompilerParams(vmem_limit_bytes=VLIM * 1024 * 1024)


def tables():
    half = DIM // 2
    frequency = (THETA ** (-(np.arange(half) * 2.0 / DIM))).astype(np.float32)
    angles = np.arange(KEYS, dtype=np.float32)[:, None] * frequency[None, :]
    cosine = np.cos(angles.astype(np.float64)).astype(np.float32)
    sine = np.sin(angles.astype(np.float64)).astype(np.float32)
    return np.concatenate([cosine, cosine, -sine, sine], axis=1)


def dot(left, right, left_dim, right_dim):
    return lax.dot_general(
        left, right, (((left_dim,), (right_dim,)), ((), ())), preferred_element_type=F32
    )


def picker(order_ref):
    rows = lax.broadcasted_iota(jnp.int32, (TOK, TOK), 0)
    return jnp.where(rows == order_ref[...], 1.0, 0.0).astype(BF)


def slot_rows(slot):
    place = lax.axis_index("dp") ^ slot
    return pl.ds(pl.multiple_of(place * ROWS, ROWS), ROWS)


def kv_pick(order_ref, k_ref, v_ref, *rest):
    outs, rows_ref = rest[:N_DP], rest[N_DP]
    chosen = picker(order_ref)
    keys = dot(chosen, k_ref[...], 0, 0).astype(BF)
    vals = dot(chosen, v_ref[...], 0, 0).astype(BF)
    for head in range(KV):
        rows_ref[:, head * PAIR : head * PAIR + DIM] = keys[:, head * DIM : (head + 1) * DIM]
        rows_ref[:, head * PAIR + DIM : (head + 1) * PAIR] = vals[:, head * DIM : (head + 1) * DIM]
    for slot in range(N_DP):
        outs[slot][...] = rows_ref[slot_rows(slot), :]


def one_pick(order_ref, array_ref, *rest):
    outs, rows_ref = rest[:N_DP], rest[N_DP]
    rows_ref[...] = dot(picker(order_ref), array_ref[...], 0, 0).astype(BF)
    for slot in range(N_DP):
        outs[slot][...] = rows_ref[slot_rows(slot), :]


def kv_join(doc_ref, *rest):
    slots, out_ref = rest[:N_DP], rest[N_DP]
    for slot in range(N_DP):
        out_ref[slot_rows(slot), :] = slots[slot][...]
    width = out_ref.shape[1]
    out_ref[TOK:, :] = jnp.full((ID_ROWS, width), doc_ref[0, 0], jnp.int32).astype(F32).astype(BF)


def same_docs(doc_ref, shards):
    own = doc_ref[0, 0].astype(F32)
    place = lax.axis_index("cp")
    flags = []
    for back in range(1, REACH + 1):
        near = jnp.max(shards[back][TOK : TOK + ID_ROWS, 0:DIM].astype(F32))
        flags.append(jnp.where((near == own) & (place >= back), 1, 0).astype(jnp.int32))
    return flags


def flip_angles(table_ref, block):
    first = pl.multiple_of(block * TOK, TOK)
    second = pl.multiple_of(block * TOK + KEYS, TOK)
    return table_ref[:, pl.ds(first, TOK)], table_ref[:, pl.ds(second, TOK)]


def columns(head, width, at=0, size=None):
    return pl.ds(pl.multiple_of(head * width + at, DIM), width if size is None else size)


def half_swap(array):
    return jnp.concatenate([array[DIM // 2 :], array[: DIM // 2]], axis=0)


def angles_of(table_ref, block):
    rows = table_ref[pl.ds(pl.multiple_of(block * TOK, TOK), TOK), :]
    return rows[:, :DIM], rows[:, DIM:]


def turn(vectors, cosine, sine):
    return vectors * cosine + pltpu.roll(vectors, DIM // 2, 1) * sine


def turn_back(vectors, cosine, sine):
    return vectors * cosine - pltpu.roll(vectors, DIM // 2, 1) * sine


def unit_of(raw):
    inv_norm = lax.rsqrt(jnp.mean(raw * raw, axis=-1, keepdims=True) + EPSILON)
    return raw * inv_norm, inv_norm


def query_unit(*refs):
    slots = refs[:N_DP]
    table_ref, flip_ref, unit_ref, norm_ref, table_out, flip_out, rows_ref = refs[N_DP:]
    table_out[...] = table_ref[...]
    flip_out[...] = flip_ref[...]
    for slot in range(N_DP):
        rows_ref[slot_rows(slot), :] = slots[slot][...]
    for at in range(0, GROUP * DIM, DIM):
        raw = rows_ref[:, at : at + DIM].astype(F32).T
        inv_norm = lax.rsqrt(jnp.mean(raw * raw, axis=0, keepdims=True) + EPSILON)
        unit_ref[:, at : at + DIM] = raw * inv_norm
        norm_ref[:, at : at + DIM] = jnp.broadcast_to(inv_norm, (8, DIM))


def forward(doc_ref, *rest):
    unitq_ref = rest[0]
    shards = rest[1 : REACH + 2]
    table_ref, flip_ref, gq_ref, gk_ref = rest[REACH + 2 : REACH + 6]
    out_ref, again_ref, prob_ref, query_ref, rot_ref, unit_ref, place_ref = rest[REACH + 6 :]
    flags = same_docs(doc_ref, shards)
    block = flags[0] + flags[1] + flags[2] + flags[3]
    place_ref[0, 0] = block
    gain_q = jnp.broadcast_to(gq_ref[...], (TOK, DIM)).T
    gain_k = gk_ref[...]
    own_cos, own_sin = flip_angles(flip_ref, block)
    levels = [jnp.where(flags[back - 1] > 0, 0.0, NEGATIVE) for back in range(REACH, 0, -1)]
    key = lax.broadcasted_iota(jnp.int32, (TOK, TILE), 0)
    query = lax.broadcasted_iota(jnp.int32, (TOK, TILE), 1) & (TOK - 1)
    causal = key <= query

    @pl.loop(0, KV)
    def each(head):
        key_rot, key_val = [], []
        for at, back in enumerate(range(REACH, -1, -1)):
            cosine, sine = angles_of(table_ref, jnp.maximum(block - back, 0))
            unit, _ = unit_of(shards[back][:TOK, columns(head, PAIR, 0, DIM)].astype(F32))
            turned = turn(unit * gain_k, cosine, sine).astype(BF)
            unit_ref[blocks[at], columns(head, DIM)] = unit
            rot_ref[blocks[at], columns(head, DIM)] = turned
            key_rot.append(turned)
            key_val.append(shards[back][:TOK, columns(head, PAIR, DIM, DIM)])
        rot_f = jnp.concatenate(key_rot, axis=0)
        val_t = jnp.concatenate(key_val, axis=0).T
        heads = TILE // TOK

        def ready(first):
            places = [(first + j) * DIM for j in range(heads)]
            turned = []
            for at in places:
                scaled = unitq_ref[:, columns(head, HALF, at, DIM)] * gain_q
                query_t = scaled * own_cos + half_swap(scaled) * own_sin
                turned.append(query_t.astype(BF))
                query_ref[:, columns(head, HALF, at, DIM)] = query_t.T.astype(BF)
            return places, dot(rot_f, jnp.concatenate(turned, axis=1), 1, 0)

        def soft(state):
            places, scores = state
            last = jnp.where(causal, scores[blocks[REACH]], NEGATIVE)
            parts = [scores[blocks[at]] for at in range(REACH)] + [last]
            tops = [jnp.max(part, axis=0, keepdims=True) for part in parts]
            top = tops[REACH]
            for at in range(REACH):
                top = jnp.maximum(top, tops[at] + levels[at])
            top = top * (INV_ROOT * LOG2E)
            weights, total = [], 0.0
            for at in range(REACH + 1):
                shift = top if at == REACH else top - levels[at]
                weight = jnp.exp2(parts[at] * (INV_ROOT * LOG2E) - shift)
                total = total + jnp.sum(weight, axis=0, keepdims=True)
                weights.append(weight)
            inverse = 1.0 / total
            for at in range(REACH + 1):
                prob_ref[blocks[at], columns(head, HALF, places[0], TILE)] = weights[at] * inverse
            weights = jnp.concatenate(weights, axis=0).astype(BF)
            out_t = dot(val_t, weights, 1, 0) / total
            for j, at in enumerate(places):
                out = out_t[:, j * TOK : (j + 1) * TOK].T.astype(BF)
                out_ref[:, columns(head, HALF, at, DIM)] = out
                again_ref[:, columns(head, HALF, at, DIM)] = out

        count = GROUP // heads
        states = {}
        for turn_at in range(count + LAG):
            if turn_at < count:
                states[turn_at] = ready(turn_at * heads)
            if turn_at >= LAG:
                soft(states.pop(turn_at - LAG))


def backward(place_ref, *rest):
    slots = rest[:N_DP]
    shards = rest[N_DP : N_DP + REACH + 1]
    out_ref, prob_ref, query_ref, unit_ref, table_ref = rest[N_DP + REACH + 1 : N_DP + REACH + 6]
    outs = rest[N_DP + REACH + 6 :]
    ds_ref, own_ref = outs[:2]
    part_refs = outs[2 : 2 + REACH]
    gain_ref, rows_ref = outs[2 + REACH :]
    block = place_ref[0, 0]

    gain_ref[...] = jnp.zeros_like(gain_ref)

    @pl.loop(0, KV)
    def each(head):
        for slot in range(N_DP):
            rows_ref[slot_rows(slot), :] = slots[slot][:, columns(head, HALF)]
        val_b = jnp.concatenate([shards[back][:TOK, columns(head, PAIR, DIM, DIM)] for back in range(REACH, -1, -1)], axis=0)
        heads = TILE // TOK

        def ready(first):
            places = [(first + j) * DIM for j in range(heads)]
            grads = [rows_ref[:, at : at + DIM] for at in places]
            grad = jnp.concatenate(grads, axis=0)
            deltas = []
            for at, own in zip(places, grads):
                both = own.astype(F32) * out_ref[:, columns(head, HALF, at, DIM)].astype(F32)
                deltas.append(jnp.sum(both.T, axis=0, keepdims=True))
            return places, grad, jnp.concatenate(deltas, axis=1), dot(val_b, grad, 1, 1)

        def back(state, sums):
            places, grad, delta, dprob = state
            span = columns(head, HALF, places[0], TILE)
            probs = prob_ref[:, span]
            dscore = (probs * (dprob - delta)).astype(BF)
            ds_ref[:, span] = dscore
            query = jnp.concatenate([query_ref[:, columns(head, HALF, at, DIM)] for at in places], axis=0)
            dk = dot(dscore, query, 1, 0)
            dv = dot(probs.astype(BF), grad, 1, 0)
            return (dk, dv) if sums is None else (sums[0] + dk, sums[1] + dv)

        count = GROUP // heads
        states, sums = {}, None
        for turn_at in range(count + LAG):
            if turn_at < count:
                states[turn_at] = ready(turn_at * heads)
            if turn_at >= LAG:
                sums = back(states.pop(turn_at - LAG), sums)
        dk_total, dv_total = sums
        gk_total = jnp.zeros((8, DIM), F32)
        for at, back_by in enumerate(range(REACH, -1, -1)):
            cosine, sine = angles_of(table_ref, jnp.maximum(block - back_by, 0))
            dk_part = dk_total[blocks[at]] * INV_ROOT
            dkn = turn_back(dk_part, cosine, sine)
            gk_total = gk_total + jnp.sum((dkn * unit_ref[blocks[at], columns(head, DIM)]).reshape(TOK // 8, 8, DIM), axis=0)
            target = own_ref if back_by == 0 else part_refs[back_by - 1]
            target[:, columns(head, PAIR, 0, DIM)] = dk_part.astype(target.dtype)
            target[:, columns(head, PAIR, DIM, DIM)] = dv_total[blocks[at]].astype(target.dtype)
        gain_ref[...] += gk_total


def query_back(place_ref, unit_ref, norm_ref, ds_ref, rot_ref, flip_ref, gq_ref, gk_ref, dq_ref, gain_ref, sum_ref):
    sum_ref[...] = jnp.zeros_like(sum_ref)
    gain_q = jnp.broadcast_to(gq_ref[...], (TOK, DIM)).T
    cosine, sine = flip_angles(flip_ref, place_ref[0, 0])

    @pl.loop(0, KV)
    def each(head):
        rot_t = rot_ref[:, columns(head, DIM)].T
        total = jnp.zeros((DIM, TOK), F32)
        for first in range(0, GROUP * DIM, TILE):
            both = dot(rot_t, ds_ref[:, columns(head, HALF, first, TILE)], 1, 0) * INV_ROOT
            for at in range(first, first + TILE, TOK):
                dq_t = both[:, at - first : at - first + TOK]
                unit = unit_ref[:, columns(head, HALF, at, DIM)]
                dqn = dq_t * cosine - half_swap(dq_t) * sine
                total = total + dqn * unit
                scaled = dqn * gain_q
                inner = jnp.mean(scaled * unit, axis=0, keepdims=True)
                back = norm_ref[0:1, columns(head, HALF, at, DIM)] * (scaled - unit * inner)
                dq_ref[:, columns(head, HALF, at, DIM)] = back.T.astype(BF)
        sum_ref[...] += total

    spread = (8, DIM)
    by_query = jnp.sum(sum_ref[...].T, axis=0, keepdims=True)
    by_key = jnp.sum(gk_ref[...], axis=0, keepdims=True)
    gain_ref[:, :DIM] = jnp.broadcast_to(by_query, spread)
    gain_ref[:, DIM:] = jnp.broadcast_to(by_key, spread)


def finish(place_ref, own_ref, *rest):
    parts = rest[:REACH]
    kv_ref, table_ref, gk_ref, every_ref, dk_ref, dv_ref, gq_out, gk_out = rest[REACH:]
    sums = jnp.sum(every_ref[...], axis=0, keepdims=True) * (1.0 / math.sqrt(TOK * N_DP * N_CP))
    gq_out[...] = sums[:, :DIM]
    gk_out[...] = sums[:, DIM:]
    cosine, sine = angles_of(table_ref, place_ref[0, 0])
    gain_k = gk_ref[...]
    for head in range(KV):
        left = head * PAIR
        both = own_ref[:, left : left + PAIR]
        for part in parts:
            both = both + part[:, left : left + PAIR].astype(F32)
        unit, inv_norm = unit_of(kv_ref[:TOK, left : left + DIM].astype(F32))
        scaled = turn_back(both[:, :DIM], cosine, sine) * gain_k
        inner = jnp.mean(scaled * unit, axis=-1, keepdims=True)
        dk_ref[:, head * DIM : (head + 1) * DIM] = (inv_norm * (scaled - unit * inner)).astype(BF)
        dv_ref[:, head * DIM : (head + 1) * DIM] = both[:, DIM:].astype(BF)


def swap(array, slot):
    return lax.ppermute(array, "dp", [(j, j ^ slot) for j in range(N_DP)])


def shifted(array, by):
    return lax.ppermute(array, "cp", [(j, (j + by) % N_CP) for j in range(N_CP)])


def shape(*dims, dtype=BF):
    return jax.ShapeDtypeStruct(dims, dtype)


def body(q_raw, k_raw, values, loss_grad, send_order, doc_blocks, gain_q, gain_k):
    table_np = tables()
    table = jnp.asarray(table_np)
    flipped = jnp.asarray(np.concatenate([table_np[:, :DIM].T, table_np[:, DIM:].T], axis=1))
    gain_q = gain_q.reshape(1, DIM)
    gain_k = gain_k.reshape(1, DIM)
    kv_slots = pl.pallas_call(
        kv_pick,
        out_shape=[shape(ROWS, KV * PAIR)] * N_DP,
        in_specs=[VMEM] * 3,
        out_specs=[VMEM] * N_DP,
        scratch_shapes=[pltpu.VMEM((TOK, KV * PAIR), BF)],
        compiler_params=pltpu.CompilerParams(vmem_limit_bytes=62 * 1024 * 1024),
        name="kv_pick",
    )(send_order, k_raw, values)
    kv_slots = [kv_slots[0]] + [swap(kv_slots[slot], slot) for slot in range(1, N_DP)]
    half = GROUP * DIM
    def pick_rows(array, name):
        return pl.pallas_call(
            one_pick,
            grid=(KV,),
            out_shape=[shape(ROWS, KV * half)] * N_DP,
            in_specs=[
                pl.BlockSpec((1, TOK), lambda h: (0, 0)),
                pl.BlockSpec((TOK, half), lambda h: (0, h)),
            ],
            out_specs=[pl.BlockSpec((ROWS, half), lambda h: (0, h))] * N_DP,
            scratch_shapes=[pltpu.VMEM((TOK, half), BF)],
            compiler_params=PARAMS,
            name=name,
        )(send_order, array)

    picked = list(pick_rows(q_raw, "q_pick")) + list(pick_rows(loss_grad, "g_pick"))
    kv_own = pl.pallas_call(
        kv_join,
        out_shape=shape(TOK + ID_ROWS, KV * PAIR),
        in_specs=[SMEM] + [VMEM] * N_DP,
        out_specs=VMEM,
        compiler_params=PARAMS,
        name="kv_join",
    )(doc_blocks, *kv_slots)
    one = shifted(kv_own, 1)
    shards = [kv_own, one, shifted(kv_own, 2), shifted(one, 2), shifted(kv_own, 4)]
    q_slots = [picked[0]] + [swap(picked[slot], slot) for slot in range(1, N_DP)]
    g_slots = [picked[N_DP]] + [swap(picked[N_DP + slot], slot) for slot in range(1, N_DP)]
    whole = lambda h: (0, 0)
    by_head = lambda h: (0, h)
    slot_specs = [pl.BlockSpec((ROWS, half), by_head)] * N_DP
    shard_specs = [pl.BlockSpec((TOK + ID_ROWS, PAIR), by_head)] * (REACH + 1)
    table_specs = [pl.BlockSpec((KEYS, 2 * DIM), whole)]
    rows_spec = pl.BlockSpec((TOK, half), by_head)
    keys_spec = pl.BlockSpec((KEYS, DIM), by_head)
    square_spec = pl.BlockSpec((KEYS, half), by_head)
    flip_specs = [pl.BlockSpec((DIM, 2 * KEYS), whole)]
    gain_spec = pl.BlockSpec((1, DIM), whole)
    norm_spec = pl.BlockSpec((8, half), by_head)
    part = KEYS // KV
    table_part = pl.BlockSpec((part, 2 * DIM), lambda h: (h, 0))
    flip_part = pl.BlockSpec((DIM // KV, 2 * KEYS), lambda h: (h, 0))
    units, norms, table, flipped = pl.pallas_call(
        query_unit,
        grid=(KV,),
        out_shape=[
            shape(DIM, KV * half, dtype=F32),
            shape(8, KV * half, dtype=F32),
            shape(KEYS, 2 * DIM, dtype=F32),
            shape(DIM, 2 * KEYS, dtype=F32),
        ],
        in_specs=slot_specs + [table_part, flip_part],
        out_specs=[rows_spec, norm_spec, table_part, flip_part],
        scratch_shapes=[pltpu.VMEM((TOK, half), BF)],
        compiler_params=PARAMS,
        name="query_unit",
    )(*q_slots, table, flipped)
    attn_out, out_again, probs, queries, keys_rot, keys_unit, place = pl.pallas_call(
        forward,
        out_shape=[
            shape(TOK, KV * half),
            shape(TOK, KV * half),
            shape(KEYS, KV * half, dtype=F32),
            shape(TOK, KV * half),
            shape(KEYS, KV * DIM),
            shape(KEYS, KV * DIM, dtype=F32),
            shape(1, 1, dtype=jnp.int32),
        ],
        in_specs=[SMEM] + [VMEM] * (REACH + 6),
        out_specs=[VMEM] * 6 + [SMEM],
        compiler_params=PARAMS,
        name="forward",
    )(doc_blocks, units, *shards, table, flipped, gain_q, gain_k)
    results = pl.pallas_call(
        backward,
        out_shape=[shape(KEYS, KV * half), shape(TOK, KV * PAIR, dtype=F32)]
        + [shape(TOK, KV * PAIR)] * REACH
        + [shape(8, DIM, dtype=F32)],
        in_specs=[SMEM] + [VMEM] * (N_DP + REACH + 6),
        out_specs=[VMEM] * (3 + REACH),
        scratch_shapes=[pltpu.VMEM((TOK, half), BF)],
        compiler_params=PARAMS,
        name="backward",
    )(place, *g_slots, *shards, out_again, probs, queries, keys_unit, table)
    dscores, dkv_own = results[:2]
    gk_rows = results[2 + REACH]
    parts = [shifted(results[1 + back], -back) for back in (4, 2, 3, 1)]

    def query_side(operands):
        place, units, norms, dscores, keys_rot, gk_rows = operands
        dq_raw, gains = pl.pallas_call(
            query_back,
            out_shape=[shape(TOK, KV * half), shape(8, 2 * DIM, dtype=F32)],
            in_specs=[SMEM] + [VMEM] * 7,
            out_specs=[VMEM] * 2,
            scratch_shapes=[pltpu.VMEM((DIM, TOK), F32)],
            compiler_params=PARAMS,
            name="query_back",
        )(place, units, norms, dscores, keys_rot, flipped, gain_q, gk_rows)
        gains = gains[0:1] + swap(gains, 1)[0:1]
        gains = jnp.broadcast_to(gains, (2 * N_CP, 2 * DIM))
        groups = [
            [(2 * chip + core) * N_CP + place for chip in range(2) for place in range(N_CP)]
            for core in range(2)
        ]
        return dq_raw, lax.all_to_all(
            gains, ("dp", "cp"), 0, 0, tiled=True, axis_index_groups=groups
        )

    def nothing(operands):
        return jnp.zeros((TOK, KV * half), BF), jnp.zeros((2 * N_CP, 2 * DIM), F32)

    dq_raw, everyone = lax.cond(
        place[0, 0] >= 0, query_side, nothing, (place, units, norms, dscores, keys_rot, gk_rows)
    )
    dk_raw, dv_out, dgain_q, dgain_k = pl.pallas_call(
        finish,
        out_shape=[shape(TOK, KV * DIM)] * 2 + [shape(1, DIM, dtype=F32)] * 2,
        in_specs=[SMEM] + [VMEM] * (REACH + 5),
        out_specs=[VMEM] * 4,
        compiler_params=PARAMS,
        name="finish",
    )(place, dkv_own, *parts, kv_own, table, gain_k, everyone)
    return attn_out, dq_raw, dk_raw, dv_out, dgain_q.reshape(DIM), dgain_k.reshape(DIM)


def solution(mesh):
    rows = P(("dp", "cp"), None)
    return jax.shard_map(
        body,
        mesh=mesh,
        in_specs=(rows, rows, rows, rows, rows, P("dp", "cp"), P(), P()),
        out_specs=(rows, rows, rows, rows, P(), P()),
        check_vma=False,
    )
```
